128 devices in a mesh: fsdp: 16 (over x_hi, z, core), tp: 8 (over y, x_lo).
Axes of the slice: x: 4 (x_hi: 2, x_lo: 2; x = x_hi * 2 + x_lo), y: 4, z: 4, core: 2. Of those that a mesh axis runs over, the one named last changes fastest.
Arguments:
- token_ids: int32 [2, 2560], replicated, may hold values from 0 to 76031
- embedding: bfloat16 [76032, 8192], P('fsdp', 'tp'), may hold values from -6 to 6
- cache_lengths: int32 [2560], P('fsdp'), may hold values from 2 to 128, as said below
- q_weight: bfloat16 [8192, 8192], P(('fsdp', 'tp')), may hold values from -6 to 6
- q_bias: bfloat16 [8192], P('tp'), may hold values from -10 to 10
- kv_bias: bfloat16 [2, 1024], P(None, 'tp'), may hold values from -3 to 3
- kv_master: float32 [8192, 2, 1024], P(('fsdp', 'tp')), may hold values from -6 to 6
- kv_moment1: float32 [8192, 2, 1024], P(('fsdp', 'tp')), may hold values from -0.6 to 0.6
- kv_moment2: float32 [8192, 2, 1024], P(('fsdp', 'tp')), may hold values from 0.01 to 4
- kv_grad: bfloat16 [8192, 2, 1024], P(('fsdp', 'tp')), may hold values from -6 to 6
- k_cache: bfloat16 [2560, 128, 1024], P('fsdp', None, 'tp'), may hold values from -16 to 16
- v_cache: bfloat16 [2560, 128, 1024], P('fsdp', None, 'tp'), may hold values from -6 to 6
Outputs:
- context: bfloat16 [2, 2560, 8192], P(None, 'fsdp', 'tp')
- kv_master_new: float32 [8192, 2, 1024], P(('fsdp', 'tp'))
- kv_moment1_new: float32 [8192, 2, 1024], P(('fsdp', 'tp'))
- kv_moment2_new: float32 [8192, 2, 1024], P(('fsdp', 'tp'))
The draws below stay inside these ranges and needn't reach their ends.
Inputs may be any that keep to these rules, and one draw needn't show every extreme that they name: Row r's cache holds keys and values at its first cache_lengths[r] positions only; some row holds 128.
All inputs are finite; a program needn't handle non-finite values.
Results may differ from the reference program's by a relative error of at most 0.02.
Values may be sent and summed in bfloat16 or wider, within the bound.
No kernel may reach another device: no remote copies, remote signals or barrier semaphores. Data moves between devices by JAX's collectives and lax.ppermute only.
A program may use at most 128 MiB of HBM per device.

```python
import math
import jax
import jax.numpy as jnp
import numpy as np
from jax import lax

D = 8192
Q_HEADS = 64
KV_HEADS = 8
HEAD = 128
VOCAB = 76032
CACHE_LEN = 128
ADAM_STEP = 10
ROWS = 2560
Q_WIDTH = 8192
KV_WIDTH = 1024


def draw_q_bias(key, part):
    key = jax.random.fold_in(key, 11)
    values = 0.5 * jax.random.normal(key, (Q_HEADS, HEAD), jnp.float32)
    return jnp.clip(values, -10.0, 10.0).reshape(Q_HEADS * HEAD).astype(jnp.bfloat16)


def draw_k_cache(key, part):
    key = jax.random.fold_in(key, 23)
    base_key = jax.random.fold_in(key, 0)
    values = jnp.clip(jax.random.normal(base_key, (ROWS, CACHE_LEN, KV_HEADS, HEAD), jnp.float32), -6.0, 6.0)
    return values.reshape(ROWS, CACHE_LEN, KV_HEADS * HEAD).astype(jnp.bfloat16)


def draw_cache_lengths(key, part):
    key = jax.random.fold_in(key, 37)
    first_key, second_key = jax.random.split(key)
    lengths = jax.random.randint(first_key, (ROWS,), 2, CACHE_LEN + 1)
    longest = jax.random.randint(second_key, (), 0, ROWS)
    return jnp.where(jnp.arange(ROWS) == longest, CACHE_LEN, lengths).astype(jnp.int32)


def with_ends(result, stream_key, low, largest):
    shape = result.shape
    spot = [jax.random.randint(jax.random.fold_in(stream_key, axis), (), 0, shape[axis]) for axis in range(len(shape))]
    result = result.at[tuple(spot)].set(low)
    longest = shape.index(max(shape))
    spot[longest] = (spot[longest] + 1) % shape[longest]
    return result.at[tuple(spot)].set(largest)


def level_of(rng, extent, pieces, smallest, largest):
    def one(position, parts):
        heights = jax.random.uniform(jax.random.fold_in(jax.random.fold_in(rng, 6), position), (parts,), jnp.float32, smallest / len(pieces), largest / len(pieces))
        return jnp.repeat(jnp.exp(heights), extent[position] // parts).reshape((-1,) + (1,) * (len(extent) - position - 1))

    loudness = one(*pieces[0])
    for cut in pieces[1:]:
        loudness = loudness * one(*cut)
    return loudness


def skewed_wide(own_key, extent, amount, slope):
    portions = [min(1 << octave, amount + 1 - (1 << octave)) * (1 << 20) // math.isqrt((1 << octave) ** slope) + 1 for octave in range((amount + 1).bit_length()) if 1 << octave <= amount]
    deviation = 1 + sum(portions) // (1 << 30)
    listing = np.cumsum(np.array([max(1, weight // deviation) for weight in portions]))
    ticket = jax.random.randint(jax.random.fold_in(own_key, 1), extent, 0, int(listing[len(portions) - 1]))
    start = jnp.left_shift(1, jnp.searchsorted(jnp.asarray(listing, jnp.int32), ticket, side="right").astype(jnp.int32))
    grade = start - 1 + jax.random.randint(jax.random.fold_in(own_key, 4), extent, 0, 1 << 30) % jnp.minimum(start, amount + 1 - start)
    return jax.random.permutation(jax.random.fold_in(own_key, 2), amount)[grade].astype(jnp.int32)


def normal_values(key, dims, deviation, limit, pieces=(), held_as=jnp.bfloat16):
    drawn = jax.random.normal(key, dims, jnp.float32) * deviation
    if len(pieces) > 0:
        drawn = level_of(key, dims, pieces, -0.22, 0.18) * drawn
    return jnp.clip(drawn, min=-limit, max=limit).astype(held_as)


def setup_inputs(seed: int = 0) -> dict:
    splits = jax.random.split(jax.random.key(seed), 13)
    return {
        "token_ids": with_ends(skewed_wide(splits[0], (2, ROWS), VOCAB, 2), jax.random.fold_in(splits[0], 3), 0, VOCAB - 1).astype(jnp.int32),
        "embedding": normal_values(splits[1], (VOCAB, D), 1.0, 6.0, ((0, 16), (1, 8))),
        "cache_lengths": draw_cache_lengths(jax.random.fold_in(splits[12], 71), 0),
        "q_weight": normal_values(splits[3], (D, Q_WIDTH), 1.0, 6.0, ((0, 128),)),
        "q_bias": draw_q_bias(jax.random.fold_in(splits[12], 71), 0),
        "kv_bias": normal_values(splits[5], (2, KV_WIDTH), 0.5, 3.0, ((1, 8),)),
        "kv_master": normal_values(splits[6], (D, 2, KV_WIDTH), 1.0, 6.0, ((0, 128),), jnp.float32),
        "kv_moment1": normal_values(splits[7], (D, 2, KV_WIDTH), 0.1, 0.6, ((0, 128),), jnp.float32),
        "kv_moment2": jnp.clip(jnp.exp(math.log(4.0) - 5.9914646 * jax.random.uniform(splits[8], (D, 2, KV_WIDTH), jnp.float32) ** level_of(splits[8], (D, 2, KV_WIDTH), ((0, 128),), -0.2, 0.2)), 0.01, 4.0),
        "kv_grad": normal_values(splits[9], (D, 2, KV_WIDTH), 1.0, 6.0, ((0, 128),)),
        "k_cache": draw_k_cache(jax.random.fold_in(splits[12], 71), 0),
        "v_cache": normal_values(splits[11], (ROWS, CACHE_LEN, KV_WIDTH), 1.0, 6.0, ((0, 16), (2, 8))),
    }


def adamw_update(master, moment1, moment2, gradient):
    gradient = gradient.astype(jnp.float32)
    moment1_new = 0.9 * moment1 + 0.1 * gradient
    moment2_new = 0.95 * moment2 + 0.05 * gradient * gradient
    first_fix = 1.0 - 0.9 ** ADAM_STEP
    second_fix = 1.0 - 0.95 ** ADAM_STEP
    update = moment1_new / first_fix / (jnp.sqrt(moment2_new / second_fix) + 1e-08)
    master_new = master - 0.01 * (update + 0.1 * master)
    return (master_new, moment1_new, moment2_new)

def rotate_half(field, positions):
    half = field.shape[-1] // 2
    freqs = jnp.exp(jnp.arange(half, dtype=jnp.float32) * (-math.log(1000000.0) / half))
    angles = positions[:, :, None].astype(jnp.float32) * freqs
    cosine = jnp.cos(angles)[:, :, None, :]
    sine = jnp.sin(angles)[:, :, None, :]
    first = field[..., :half]
    second = field[..., half:]
    return jnp.concatenate([first * cosine - second * sine, second * cosine + first * sine], axis=-1)

def reference(token_ids, embedding, cache_lengths, q_weight, q_bias, kv_bias, kv_master, kv_moment1, kv_moment2, kv_grad, k_cache, v_cache):
    embedded = embedding[token_ids]
    widened = embedded.astype(jnp.float32)
    stats = lax.optimization_barrier(jnp.mean(widened * widened, axis=-1, keepdims=True))
    normed = (widened * lax.rsqrt(stats + 1e-06)).astype(jnp.bfloat16)
    master_new, moment1_new, moment2_new = adamw_update(kv_master, kv_moment1, kv_moment2, kv_grad)
    rollout = master_new.astype(jnp.bfloat16).reshape(D, 2 * KV_WIDTH)
    tokens = normed.reshape(2 * ROWS, D)
    query_raw = jnp.dot(tokens, q_weight, preferred_element_type=jnp.float32) / math.sqrt(D) + q_bias.astype(jnp.float32)
    pair_raw = jnp.dot(tokens, rollout, preferred_element_type=jnp.float32) / math.sqrt(D) + kv_bias.reshape(2 * KV_WIDTH).astype(jnp.float32)
    positions = cache_lengths[None, :] + jnp.arange(2, dtype=jnp.int32)[:, None]
    queries = rotate_half(query_raw.reshape(2, ROWS, Q_HEADS, HEAD), positions).astype(jnp.bfloat16)
    new_keys = rotate_half(pair_raw[:, :KV_WIDTH].reshape(2, ROWS, KV_HEADS, HEAD), positions).astype(jnp.bfloat16)
    new_values = pair_raw[:, KV_WIDTH:].reshape(2, ROWS, KV_HEADS, HEAD).astype(jnp.bfloat16)
    grouped = queries.reshape(2, ROWS, KV_HEADS, Q_HEADS // KV_HEADS, HEAD).astype(jnp.float32)
    cache_keys = k_cache.reshape(ROWS, CACHE_LEN, KV_HEADS, HEAD).astype(jnp.float32)
    cache_values = v_cache.reshape(ROWS, CACHE_LEN, KV_HEADS, HEAD).astype(jnp.float32)
    cache_scores = jnp.einsum('srkgd,rlkd->srkgl', grouped, cache_keys) / math.sqrt(HEAD)
    new_scores = jnp.einsum('srkgd,urkd->srkgu', grouped, new_keys.astype(jnp.float32)) / math.sqrt(HEAD)
    cache_valid = (jnp.arange(CACHE_LEN)[None, :] < cache_lengths[:, None])[None, :, None, None, :]
    new_valid = (jnp.arange(2)[None, :] <= jnp.arange(2)[:, None])[:, None, None, None, :]
    cache_scores = jnp.where(cache_valid, cache_scores, -1e+30)
    new_scores = jnp.where(new_valid, new_scores, -1e+30)
    peak = jnp.maximum(lax.optimization_barrier(jnp.max(cache_scores, axis=-1, keepdims=True)), lax.optimization_barrier(jnp.max(new_scores, axis=-1, keepdims=True)))
    cache_exp = jnp.exp(cache_scores - peak)
    new_exp = jnp.exp(new_scores - peak)
    total = lax.optimization_barrier(jnp.sum(cache_exp, axis=-1, keepdims=True)) + lax.optimization_barrier(jnp.sum(new_exp, axis=-1, keepdims=True))
    cache_weights = (cache_exp / total).astype(jnp.bfloat16).astype(jnp.float32)
    new_weights = (new_exp / total).astype(jnp.bfloat16).astype(jnp.float32)
    context = jnp.einsum('srkgl,rlkd->srkgd', cache_weights, cache_values)
    context = context + jnp.einsum('srkgu,urkd->srkgd', new_weights, new_values.astype(jnp.float32))
    context = context.reshape(2, ROWS, Q_WIDTH).astype(jnp.bfloat16)
    return (context, master_new, moment1_new, moment2_new)
```

```python
import functools
import math

import jax
import jax.numpy as jnp
from jax import lax
from jax.experimental import pallas as pl
from jax.experimental.pallas import tpu as pltpu
from jax.sharding import Mesh
from jax.sharding import PartitionSpec as P

D = 8192
HEAD = 128
ADAM_STEP = 10

NAMES = ("xh", "z", "c", "y", "xl")
SIZES = (2, 4, 2, 4, 2)
FSDP = ("xh", "z", "c")
TP = ("y", "xl")
OWNERS = 16
PAIRS = 8
ROWS = 160
TOKENS = 4 * ROWS
HALF = 512
SLOTS = 64
COLS = 1280


def pairs_of(move):
    found = []
    total = math.prod(SIZES)
    for index in range(total):
        rest, coords = index, []
        for size in reversed(SIZES):
            coords.append(rest % size)
            rest //= size
        target = 0
        for value, size in zip(move(*reversed(coords)), SIZES):
            target = target * size + value
        found.append((index, target))
    return found


def send(array, move):
    return lax.ppermute(array, NAMES, pairs_of(move))


def along_y(step):
    return lambda xh, z, c, y, xl: (xh, z, c, (y + step) % 4, xl)


def other_xl(xh, z, c, y, xl):
    return (xh, z, c, y, 1 - xl)


def other_xh(xh, z, c, y, xl):
    return (1 - xh, z, c, y, xl)


def swap_xh_core(xh, z, c, y, xl):
    return (c, z, xh, y, xl)


def adamw_update(master, moment1, moment2, gradient):
    gradient = gradient.astype(jnp.float32)
    moment1_new = 0.9 * moment1 + 0.1 * gradient
    moment2_new = 0.95 * moment2 + 0.05 * gradient * gradient
    first_fix = 1.0 - 0.9**ADAM_STEP
    second_fix = 1.0 - 0.95**ADAM_STEP
    update = moment1_new / first_fix / (jnp.sqrt(moment2_new / second_fix) + 1e-08)
    master_new = master - 0.01 * (update + 0.1 * master)
    return (master_new, moment1_new, moment2_new)


def rotation(positions):
    half = HEAD // 2
    freqs = jnp.exp(jnp.arange(half, dtype=jnp.float32) * (-math.log(1000000.0) / half))
    angles = positions[:, :, None].astype(jnp.float32) * freqs
    return jnp.cos(angles)[:, :, None, :], jnp.sin(angles)[:, :, None, :]


def rotate_half(field, cosine, sine):
    half = field.shape[-1] // 2
    first = field[..., :half]
    second = field[..., half:]
    return jnp.concatenate(
        [first * cosine - second * sine, second * cosine + first * sine], axis=-1
    )


def pack_kernel(query_ref, key_ref, value_ref, out_ref):
    out_ref[0, :, 0:1024] = query_ref[...]
    out_ref[0, :, 1024:1152] = key_ref[...]
    out_ref[0, :, 1152:1280] = value_ref[...]


def pack_columns(q_weight, keys, values):
    rows = q_weight.shape[0]
    return pl.pallas_call(
        pack_kernel,
        grid=(8,),
        in_specs=[
            pl.BlockSpec((rows, 1024), lambda t: (0, t)),
            pl.BlockSpec((rows, 128), lambda t: (0, t)),
            pl.BlockSpec((rows, 128), lambda t: (0, t)),
        ],
        out_specs=pl.BlockSpec((1, rows, COLS), lambda t: (t, 0, 0)),
        out_shape=jax.ShapeDtypeStruct((8, rows, COLS), jnp.bfloat16),
    )(q_weight, keys, values)


def project_kernel(place_ref, *refs):
    blocks = refs[:8]
    w_ref, mine_ref, other_ref, held, total, squares, sems = refs[8:]
    step = pl.program_id(0)
    copies = []
    for index in range(6):
        copies.append((pltpu.make_async_copy(blocks[index], held.at[index], sems.at[index]),))
    half = TOKENS // 2
    lower, upper = refs[6], refs[7]
    for index in range(2):
        copies.append(
            (
                pltpu.make_async_copy(
                    lower.at[index], held.at[6 + index, pl.ds(0, half)], sems.at[6 + 2 * index]
                ),
                pltpu.make_async_copy(
                    upper.at[index], held.at[6 + index, pl.ds(half, half)], sems.at[7 + 2 * index]
                ),
            )
        )

    @pl.when(step == 0)
    def _():
        for group in copies:
            for copy in group:
                copy.start()
        total[...] = jnp.zeros_like(total)
        squares[...] = jnp.zeros_like(squares)

    for index in range(8):

        @pl.when(step == index)
        def _(index=index):
            for copy in copies[index]:
                copy.wait()

    tokens = held.at[step]

    def tile(index, carry):
        columns = pl.ds(pl.multiple_of(index * 256, 256), 256)
        total[:, columns] += jnp.dot(
            tokens[...], w_ref[0, :, columns], preferred_element_type=jnp.float32
        )
        return carry

    lax.fori_loop(0, COLS // 256, tile, 0)
    for start in range(0, HALF, 128):
        part = tokens[:, start : start + 128].astype(jnp.float32)
        squares[...] += part * part

    @pl.when(step == 7)
    def _():
        xh = place_ref[8]
        own = pl.ds(pl.multiple_of(xh * half, half), half)
        partner = pl.ds(pl.multiple_of((1 - xh) * half, half), half)
        mine_ref[:, 0:COLS] = total[own, :]
        own_sum = jnp.sum(squares[own, :], axis=1, keepdims=True)
        mine_ref[:, COLS:] = jnp.broadcast_to(own_sum, (half, 128))
        other_ref[:, 0:COLS] = total[partner, :].astype(jnp.bfloat16)
        sums = jnp.sum(squares[partner, :], axis=1, keepdims=True)
        high = sums.astype(jnp.bfloat16).astype(jnp.float32)
        lanes = lax.broadcasted_iota(jnp.int32, (half, 128), 1)
        other_ref[:, COLS:] = jnp.where(lanes < 64, high, sums - high).astype(jnp.bfloat16)


def project(place, blocks, lower, upper, weights):
    half = TOKENS // 2
    anywhere = pl.BlockSpec(memory_space=pl.ANY)
    return pl.pallas_call(
        project_kernel,
        grid_spec=pltpu.PrefetchScalarGridSpec(
            num_scalar_prefetch=1,
            grid=(8,),
            in_specs=[anywhere] * 8
            + [pl.BlockSpec((1, HALF, COLS), lambda k, place: (place[k], 0, 0))],
            out_specs=[
                pl.BlockSpec((half, COLS + 128), lambda k, place: (0, 0)),
                pl.BlockSpec((half, COLS + 128), lambda k, place: (0, 0)),
            ],
            scratch_shapes=[
                pltpu.VMEM((8, TOKENS, HALF), jnp.bfloat16),
                pltpu.VMEM((TOKENS, COLS), jnp.float32),
                pltpu.VMEM((TOKENS, 128), jnp.float32),
                pltpu.SemaphoreType.DMA((10,)),
            ],
        ),
        out_shape=[
            jax.ShapeDtypeStruct((half, COLS + 128), jnp.float32),
            jax.ShapeDtypeStruct((half, COLS + 128), jnp.bfloat16),
        ],
        compiler_params=pltpu.CompilerParams(vmem_limit_bytes=48 << 20),
        cost_estimate=pl.CostEstimate(
            flops=2 * TOKENS * 4096 * COLS, bytes_accessed=20 << 20, transcendentals=0
        ),
    )(place, *blocks, lower, upper, weights)


def per_device(
    token_ids,
    embedding,
    cache_lengths,
    q_weight,
    q_bias,
    kv_bias,
    kv_master,
    kv_moment1,
    kv_moment2,
    kv_grad,
    k_cache,
    v_cache,
):
    xh, z, c = (lax.axis_index(name) for name in FSDP)
    y, xl = (lax.axis_index(name) for name in TP)
    fsdp_index = (xh * 4 + z) * 2 + c
    pair = z * 2 + c
    vocab_rows = embedding.shape[0]

    master_new, moment1_new, moment2_new = adamw_update(kv_master, kv_moment1, kv_moment2, kv_grad)
    rollout = master_new.astype(jnp.bfloat16)
    packed = pack_columns(q_weight, rollout[:, 0, :], rollout[:, 1, :])
    columns = lax.all_to_all(packed, TP, split_axis=0, concat_axis=0)
    columns = send(columns.reshape(512, COLS), swap_xh_core)
    weights = lax.all_gather(columns, ("z", "c"))

    paired = token_ids.reshape(2, 2, PAIRS, ROWS).transpose(2, 1, 0, 3).reshape(PAIRS, TOKENS)
    owners = paired // vocab_rows
    order = jnp.arange(TOKENS, dtype=jnp.int32)
    earlier = order[:, None] < order[None, :]
    same_id = paired[:, :, None] == paired[:, None, :]
    first = ~jnp.any(same_id & earlier[None], axis=1)
    first_owner = jnp.where(first, owners, -1)
    ranks = jnp.sum(
        ((first_owner[:, :, None] == owners[:, None, :]) & earlier[None]).astype(jnp.int32), axis=1
    )
    rounds = (jnp.max(jnp.where(first, ranks, 0)) + SLOTS) // SLOTS

    local = paired - fsdp_index * vocab_rows
    sent_rank = jnp.where(first_owner == fsdp_index, ranks, -1)
    own_ids = lax.dynamic_index_in_dim(paired, pair, 0, keepdims=False)
    own_first = lax.dynamic_index_in_dim(first, pair, 0, keepdims=False)
    own_ranks = lax.dynamic_index_in_dim(ranks, pair, 0, keepdims=False)
    own_owners = lax.dynamic_index_in_dim(owners, pair, 0, keepdims=False)
    got_rank = jnp.sum(
        jnp.where(
            (own_ids[:, None] == own_ids[None, :]) & own_first[:, None], own_ranks[:, None], 0
        ),
        axis=0,
    )

    def fetch(turn):
        slots = turn * SLOTS + jnp.arange(SLOTS, dtype=jnp.int32)
        wanted = jnp.sum(
            jnp.where(sent_rank[:, :, None] == slots[None, None, :], local[:, :, None], 0), axis=1
        )
        rows = embedding.at[wanted.reshape(-1)].get(mode="promise_in_bounds")
        rows = rows.reshape(PAIRS, SLOTS, 2, HALF).transpose(2, 0, 1, 3)
        rows = rows.reshape(OWNERS, SLOTS, HALF)
        rows = lax.all_to_all(rows, FSDP, split_axis=0, concat_axis=0)
        slot = got_rank - turn * SLOTS
        inside = (slot >= 0) & (slot < SLOTS)
        spot = jnp.where(inside, own_owners * SLOTS + slot, -1)
        pick = spot[:, None] == jnp.arange(OWNERS * SLOTS, dtype=jnp.int32)[None, :]
        return jnp.dot(
            pick.astype(jnp.bfloat16),
            rows.reshape(OWNERS * SLOTS, HALF),
            preferred_element_type=jnp.float32,
        ).astype(jnp.bfloat16)

    own = fetch(0)
    _, own = lax.while_loop(
        lambda state: state[0] < rounds,
        lambda state: (state[0] + 1, state[1] + fetch(state[0])),
        (jnp.int32(1), own),
    )

    half = TOKENS // 2
    across = send(own, other_xl)
    below = send(own, along_y(1))
    above = send(own, along_y(-1))
    far_low = send(below[:half], along_y(1))
    far_high = send(above[half:], along_y(-1))
    below_across = send(across, along_y(1))
    above_across = send(across, along_y(-1))
    far_low_across = send(far_low, other_xl)
    far_high_across = send(far_high, other_xl)
    members = [
        y * 2 + xl,
        y * 2 + 1 - xl,
        (y + 3) % 4 * 2 + xl,
        (y + 1) % 4 * 2 + xl,
        (y + 3) % 4 * 2 + 1 - xl,
        (y + 1) % 4 * 2 + 1 - xl,
        (y + 2) % 4 * 2 + xl,
        (y + 2) % 4 * 2 + 1 - xl,
    ]
    place = jnp.stack([member % 4 * 2 + member // 4 for member in members] + [xh]).astype(jnp.int32)
    mine, other = project(
        place,
        (own, across, below, above, below_across, above_across),
        jnp.stack([far_low, far_low_across]),
        jnp.stack([far_high, far_high_across]),
        weights,
    )
    arrived = send(other, other_xh).astype(jnp.float32)

    group_rows = ROWS
    sums = mine[:, COLS] + arrived[:, COLS] + arrived[:, COLS + 64]
    scale = lax.rsqrt(sums / D + 1e-06) / math.sqrt(D)
    bias = jnp.concatenate([q_bias, kv_bias.reshape(256)]).astype(jnp.float32)
    raw = (mine[:, :COLS] + arrived[:, :COLS]) * scale[:, None] + bias
    positions = cache_lengths[None, :] + jnp.arange(2, dtype=jnp.int32)[:, None]
    cosine, sine = rotation(positions)
    queries = rotate_half(raw[:, :1024].reshape(2, group_rows, 8, HEAD), cosine, sine).astype(
        jnp.bfloat16
    )
    new_keys = rotate_half(raw[:, 1024:1152].reshape(2, group_rows, 1, HEAD), cosine, sine).astype(
        jnp.bfloat16
    )
    new_values = raw[:, 1152:].reshape(2, group_rows, 1, HEAD).astype(jnp.bfloat16)
    grouped = queries.reshape(2, group_rows, 1, 8, HEAD)
    cache_size = k_cache.shape[1]
    cache_keys = k_cache.reshape(group_rows, cache_size, 1, HEAD)
    cache_values = v_cache.reshape(group_rows, cache_size, 1, HEAD)
    cache_scores = jnp.einsum(
        "srkgd,rlkd->srkgl", grouped, cache_keys, preferred_element_type=jnp.float32
    ) / math.sqrt(HEAD)
    new_scores = jnp.einsum(
        "srkgd,urkd->srkgu", grouped, new_keys, preferred_element_type=jnp.float32
    ) / math.sqrt(HEAD)
    cache_valid = (jnp.arange(cache_size)[None, :] < cache_lengths[:, None])[None, :, None, None, :]
    new_valid = (jnp.arange(2)[None, :] <= jnp.arange(2)[:, None])[:, None, None, None, :]
    cache_scores = jnp.where(cache_valid, cache_scores, -1e30)
    new_scores = jnp.where(new_valid, new_scores, -1e30)
    peak = jnp.maximum(
        jnp.max(cache_scores, axis=-1, keepdims=True), jnp.max(new_scores, axis=-1, keepdims=True)
    )
    cache_exp = jnp.exp(cache_scores - peak)
    new_exp = jnp.exp(new_scores - peak)
    total = jnp.sum(cache_exp, axis=-1, keepdims=True) + jnp.sum(new_exp, axis=-1, keepdims=True)
    cache_weights = (cache_exp / total).astype(jnp.bfloat16)
    new_weights = (new_exp / total).astype(jnp.bfloat16)
    context = jnp.einsum(
        "srkgl,rlkd->srkgd", cache_weights, cache_values, preferred_element_type=jnp.float32
    )
    context = context + jnp.einsum(
        "srkgu,urkd->srkgd", new_weights, new_values, preferred_element_type=jnp.float32
    )
    context = context.reshape(2, group_rows, 1024).astype(jnp.bfloat16)
    return (context, master_new, moment1_new, moment2_new)


def solution(mesh):
    parts = Mesh(mesh.devices.reshape(SIZES), NAMES)
    placed = (
        P(),
        P(FSDP, TP),
        P(FSDP),
        P(NAMES, None),
        P(TP),
        P(None, TP),
        P(NAMES, None, None),
        P(NAMES, None, None),
        P(NAMES, None, None),
        P(NAMES, None, None),
        P(FSDP, None, TP),
        P(FSDP, None, TP),
    )
    return jax.shard_map(
        per_device,
        mesh=parts,
        in_specs=placed,
        out_specs=(
            P(None, FSDP, TP),
            P(NAMES, None, None),
            P(NAMES, None, None),
            P(NAMES, None, None),
        ),
        check_vma=False,
    )
```

```python
import functools
import functools
import math

import jax
import jax.numpy as jnp
from jax import lax
from jax.experimental import pallas as pl
from jax.experimental.pallas import tpu as pltpu
from jax.sharding import Mesh
from jax.sharding import PartitionSpec as P

D = 8192
HEAD = 128
ADAM_STEP = 10

NAMES = ("xh", "z", "c", "y", "xl")
SIZES = (2, 4, 2, 4, 2)
FSDP = ("xh", "z", "c")
TP = ("y", "xl")
OWNERS = 16
PAIRS = 8
ROWS = 160
TOKENS = 4 * ROWS
HALF = 512
SLOTS = 64
PART = 512
FIRST = 768


def pairs_of(move):
    found = []
    total = math.prod(SIZES)
    for index in range(total):
        rest, coords = index, []
        for size in reversed(SIZES):
            coords.append(rest % size)
            rest //= size
        target = 0
        for value, size in zip(move(*reversed(coords)), SIZES):
            target = target * size + value
        found.append((index, target))
    return found


def send(array, move):
    return lax.ppermute(array, NAMES, pairs_of(move))


def along_y(step):
    return lambda xh, z, c, y, xl: (xh, z, c, (y + step) % 4, xl)


def other_xl(xh, z, c, y, xl):
    return (xh, z, c, y, 1 - xl)


def other_xh(xh, z, c, y, xl):
    return (1 - xh, z, c, y, xl)


def swap_xh_core(xh, z, c, y, xl):
    return (c, z, xh, y, xl)


def adamw_update(master, moment1, moment2, gradient):
    gradient = gradient.astype(jnp.float32)
    moment1_new = 0.9 * moment1 + 0.1 * gradient
    moment2_new = 0.95 * moment2 + 0.05 * gradient * gradient
    first_fix = 1.0 - 0.9**ADAM_STEP
    second_fix = 1.0 - 0.95**ADAM_STEP
    update = moment1_new / first_fix / (jnp.sqrt(moment2_new / second_fix) + 1e-08)
    master_new = master - 0.01 * (update + 0.1 * master)
    return (master_new, moment1_new, moment2_new)


def rotation(positions):
    half = HEAD // 2
    freqs = jnp.exp(jnp.arange(half, dtype=jnp.float32) * (-math.log(1000000.0) / half))
    angles = positions[:, :, None].astype(jnp.float32) * freqs
    cosine, sine = jnp.cos(angles), jnp.sin(angles)
    return jnp.concatenate([cosine, cosine], axis=-1), jnp.concatenate([-sine, sine], axis=-1)


def pack_kernel(query_ref, key_ref, value_ref, first_ref, second_ref):
    for member in range(8):
        start = member * 1024
        own = slice(member * 128, member * 128 + 128)
        first_ref[member, :, 0:PART] = query_ref[:, start : start + PART]
        first_ref[member, :, PART : PART + 128] = key_ref[:, own]
        first_ref[member, :, PART + 128 : FIRST] = value_ref[:, own]
        second_ref[member] = query_ref[:, start + PART : start + 1024]


def pack_columns(q_weight, keys, values):
    rows = q_weight.shape[0]
    whole = pl.BlockSpec(memory_space=pltpu.VMEM)
    return pl.pallas_call(
        pack_kernel,
        in_specs=[whole] * 3,
        out_specs=[whole] * 2,
        out_shape=[
            jax.ShapeDtypeStruct((8, rows, FIRST), jnp.bfloat16),
            jax.ShapeDtypeStruct((8, rows, PART), jnp.bfloat16),
        ],
        compiler_params=pltpu.CompilerParams(vmem_limit_bytes=16 << 20),
        cost_estimate=pl.CostEstimate(flops=0, bytes_accessed=3 << 20, transcendentals=0),
    )(q_weight, keys, values)


def project_kernel(place_ref, *refs):
    blocks, w_ref, mine_ref, other_ref, tokens_ref, held, total, sems = refs[:10], *refs[10:17]
    half = TOKENS // 2
    width = w_ref.shape[1]
    columns = mine_ref.shape[1] - 128
    keep = pltpu.make_async_copy(held, tokens_ref, sems.at[10])
    step = pl.program_id(0)

    @pl.when(step == 0)
    def _():
        copies = []
        for index in range(10):
            member = index if index < 6 else 6 + (index - 6) // 2
            features = pl.ds(pl.multiple_of(place_ref[member] * HALF, HALF), HALF)
            if index < 6:
                target = held.at[:, features]
            else:
                target = held.at[pl.ds((index - 6) % 2 * half, half), features]
            copies.append(pltpu.make_async_copy(blocks[index], target, sems.at[index]))
        for copy in copies:
            copy.start()
        for copy in copies:
            copy.wait()
        keep.start()

    xh = place_ref[8]
    own = pl.ds(pl.multiple_of(xh * half, half), half)
    partner = pl.ds(pl.multiple_of((1 - xh) * half, half), half)
    tile = pl.ds(pl.multiple_of(step * width, width), width)
    total[...] = jnp.dot(held[...], w_ref[...], preferred_element_type=jnp.float32)
    other_ref[:, tile] = total[partner, :].astype(jnp.bfloat16)
    mine_ref[:, tile] = total[own, :]

    @pl.when(step == 0)
    def _():
        def sums(rows):
            parts = jnp.zeros((half, 128), jnp.float32)
            for start in range(0, 8 * HALF, 128):
                part = held[rows, start : start + 128].astype(jnp.float32)
                parts += part * part
            return jnp.sum(parts, axis=1, keepdims=True)

        mine_ref[:, columns:] = jnp.broadcast_to(sums(own), (half, 128))
        partner_sums = sums(partner)
        high = partner_sums.astype(jnp.bfloat16).astype(jnp.float32)
        lanes = lax.broadcasted_iota(jnp.int32, (half, 128), 1)
        other_ref[:, columns:] = jnp.where(lanes < 64, high, partner_sums - high).astype(
            jnp.bfloat16
        )

    @pl.when(step == pl.num_programs(0) - 1)
    def _():
        keep.wait()


def project(place, blocks, weights):
    half = TOKENS // 2
    columns = weights.shape[1]
    width = columns + 128
    anywhere = pl.BlockSpec(memory_space=pltpu.HBM)
    return pl.pallas_call(
        project_kernel,
        grid_spec=pltpu.PrefetchScalarGridSpec(
            num_scalar_prefetch=1,
            grid=(columns // 256,),
            in_specs=[anywhere] * 10 + [pl.BlockSpec((8 * HALF, 256), lambda n, place: (0, n))],
            out_specs=[
                pl.BlockSpec((half, width), lambda n, place: (0, 0)),
                pl.BlockSpec((half, width), lambda n, place: (0, 0)),
                anywhere,
            ],
            scratch_shapes=[
                pltpu.VMEM((TOKENS, 8 * HALF), jnp.bfloat16),
                pltpu.VMEM((TOKENS, 256), jnp.float32),
                pltpu.SemaphoreType.DMA((11,)),
            ],
        ),
        out_shape=[
            jax.ShapeDtypeStruct((half, width), jnp.float32),
            jax.ShapeDtypeStruct((half, width), jnp.bfloat16),
            jax.ShapeDtypeStruct((TOKENS, 8 * HALF), jnp.bfloat16),
        ],
        compiler_params=pltpu.CompilerParams(vmem_limit_bytes=60 << 20),
        cost_estimate=pl.CostEstimate(
            flops=2 * TOKENS * 4096 * columns, bytes_accessed=12 << 20, transcendentals=0
        ),
    )(place, *blocks, weights)


def hold_kernel(keys, values, keys_out, values_out, sems):
    copies = []
    for index in range(5):
        rows = pl.ds(index * 32, 32)
        copies.append(pltpu.make_async_copy(keys.at[rows], keys_out.at[rows], sems.at[index]))
        copies.append(
            pltpu.make_async_copy(values.at[rows], values_out.at[rows], sems.at[5 + index])
        )
    for copy in copies:
        copy.start()
    for copy in copies:
        copy.wait()


def hold(k_cache, v_cache):
    far = pl.BlockSpec(memory_space=pltpu.HBM)
    near = pl.BlockSpec(memory_space=pltpu.VMEM)
    return pl.pallas_call(
        hold_kernel,
        in_specs=[far, far],
        out_specs=[near, near],
        out_shape=[jax.ShapeDtypeStruct(k_cache.shape, k_cache.dtype)] * 2,
        scratch_shapes=[pltpu.SemaphoreType.DMA((10,))],
        compiler_params=pltpu.CompilerParams(vmem_limit_bytes=12 << 20),
        cost_estimate=pl.CostEstimate(flops=0, bytes_accessed=20 << 20, transcendentals=0),
    )(k_cache, v_cache)


BLOCK = 32


def spread(scratch, array):
    for index in range(8):
        scratch[pl.ds(index, BLOCK, stride=8), :] = array
    return scratch[...].reshape(BLOCK, 8, HEAD)


def attend_kernel(first, *refs):
    if first:
        mine, came, bias, cosine, sine, mask, k_ref, v_ref = refs[:8]
        out, keys_out, values_out, scale_out = refs[8:12]
        work = refs[12]
        spare = refs[13:]
    else:
        mine, came, bias, cosine, sine, mask, k_ref, v_ref = refs[:8]
        keys_in, values_in, scale_in = refs[8:11]
        out = refs[12]
        work = refs[13]
        spare = refs[14:]

    def rotated(field, step):
        return field * cosine[step] + pltpu.roll(field, HEAD // 2, 1) * sine[step]

    def raw(step, start, scale):
        features = slice(start, start + HEAD)
        total = mine[step, :, features] + came[step, :, features].astype(jnp.float32)
        return total * scale + bias[:, features]

    new_keys, new_values = [], []
    for step in range(2):
        if first:
            part = came[step, :, FIRST : FIRST + 128].astype(jnp.float32)
            sums = mine[step, :, FIRST : FIRST + 128] + part + pltpu.roll(part, 64, 1)
            scale = lax.rsqrt(sums / D + 1e-06) / math.sqrt(D)
            scale_out[step] = scale
            key = rotated(raw(step, PART, scale), step).astype(jnp.bfloat16)
            value = raw(step, PART + HEAD, scale).astype(jnp.bfloat16)
            keys_out[step] = key
            values_out[step] = value
        else:
            scale = scale_in[step]
            key, value = keys_in[step], values_in[step]
        new_keys.append(key.astype(jnp.float32))
        new_values.append(value.astype(jnp.float32))
        for head in range(4):
            query = rotated(raw(step, head * HEAD, scale), step)
            work[pl.ds(step * 4 + head, BLOCK, stride=8), :] = query
    queries = work[...].reshape(BLOCK, 8, HEAD).astype(jnp.bfloat16)
    wide = queries.astype(jnp.float32)
    root = 1.0 / math.sqrt(HEAD)
    near = pl.ds(pl.multiple_of(pl.program_id(0) * BLOCK, BLOCK), BLOCK)
    scores = (
        lax.dot_general(
            queries, k_ref[near], (((2,), (2,)), ((0,), (0,))), preferred_element_type=jnp.float32
        )
        * root
        + mask[...]
    )
    second = lax.broadcasted_iota(jnp.int32, (BLOCK, 8, 1), 1) >= 4
    own = [
        jnp.sum(wide * spread(spare[u], new_keys[u]), axis=2, keepdims=True) * root
        for u in range(2)
    ]
    own[1] = jnp.where(second, own[1], -1e30)
    peak = jnp.maximum(
        jnp.max(scores, axis=2, keepdims=True), jnp.maximum(own[0], own[1])
    )
    shares = jnp.exp(scores - peak)
    own = [jnp.exp(score - peak) for score in own]
    total = jnp.sum(shares, axis=2, keepdims=True) + own[0] + own[1]
    inverse = 1.0 / total
    weights = (shares * inverse).astype(jnp.bfloat16)
    context = lax.dot_general(
        weights, v_ref[near], (((2,), (1,)), ((0,), (0,))), preferred_element_type=jnp.float32
    )
    for u in range(2):
        weight = (own[u] * inverse).astype(jnp.bfloat16).astype(jnp.float32)
        context += weight * spread(spare[2 + u], new_values[u])
    work[...] = context.reshape(BLOCK * 8, HEAD)
    for step in range(2):
        for head in range(4):
            result = work[pl.ds(step * 4 + head, BLOCK, stride=8), :]
            out[step, :, head * HEAD : (head + 1) * HEAD] = result.astype(jnp.bfloat16)


def attend(first, mine, came, bias, cosine, sine, mask, k_cache, v_cache, *more):
    width = mine.shape[-1]

    def steps(columns):
        return pl.BlockSpec((2, BLOCK, columns), lambda i: (0, i, 0))

    def rows(a, b):
        return pl.BlockSpec((BLOCK, a, b), lambda i: (i, 0, 0))

    in_specs = [
        steps(width),
        steps(width),
        pl.BlockSpec((1, bias.shape[-1]), lambda i: (0, 0)),
        steps(HEAD),
        steps(HEAD),
        rows(8, HEAD),
        pl.BlockSpec(memory_space=pltpu.VMEM),
        pl.BlockSpec(memory_space=pltpu.VMEM),
    ]
    context = jax.ShapeDtypeStruct((2, ROWS, 2 * PART), jnp.bfloat16)
    if first:
        out_specs = [steps(PART), steps(HEAD), steps(HEAD), steps(HEAD)]
        out_shape = [
            context,
            jax.ShapeDtypeStruct((2, ROWS, HEAD), jnp.bfloat16),
            jax.ShapeDtypeStruct((2, ROWS, HEAD), jnp.bfloat16),
            jax.ShapeDtypeStruct((2, ROWS, HEAD), jnp.float32),
        ]
        aliases = {}
    else:
        in_specs += [steps(HEAD), steps(HEAD), steps(HEAD), pl.BlockSpec(memory_space=pl.ANY)]
        out_specs = pl.BlockSpec((2, BLOCK, PART), lambda i: (0, i, 1))
        out_shape = context
        aliases = {11: 0}
    return pl.pallas_call(
        functools.partial(attend_kernel, first),
        grid=(ROWS // BLOCK,),
        in_specs=in_specs,
        out_specs=out_specs,
        out_shape=out_shape,
        scratch_shapes=[pltpu.VMEM((BLOCK * 8, HEAD), jnp.float32)] * 5,
        input_output_aliases=aliases,
        compiler_params=pltpu.CompilerParams(vmem_limit_bytes=24 << 20),
        cost_estimate=pl.CostEstimate(
            flops=4 * ROWS * 8 * 128 * 128, bytes_accessed=12 << 20, transcendentals=ROWS * 1024
        ),
    )(mine, came, bias, cosine, sine, mask, k_cache, v_cache, *more)


def per_device(
    token_ids,
    embedding,
    cache_lengths,
    q_weight,
    q_bias,
    kv_bias,
    kv_master,
    kv_moment1,
    kv_moment2,
    kv_grad,
    k_cache,
    v_cache,
):
    xh, z, c = (lax.axis_index(name) for name in FSDP)
    y, xl = (lax.axis_index(name) for name in TP)
    fsdp_index = (xh * 4 + z) * 2 + c
    pair = z * 2 + c
    vocab_rows = embedding.shape[0]

    queries = send(q_weight, swap_xh_core)
    master_new, moment1_new, moment2_new = adamw_update(kv_master, kv_moment1, kv_moment2, kv_grad)
    rollout = master_new.astype(jnp.bfloat16)
    rollout = jnp.concatenate([rollout[:, 0, :], rollout[:, 1, :]], axis=1)
    rollout = send(rollout, swap_xh_core)

    paired = token_ids.reshape(2, 2, PAIRS, ROWS).transpose(2, 1, 0, 3).reshape(PAIRS, TOKENS)
    owners = paired // vocab_rows
    order = jnp.arange(TOKENS, dtype=jnp.int32)
    earlier = order[:, None] < order[None, :]
    same_id = paired[:, :, None] == paired[:, None, :]
    first = ~jnp.any(same_id & earlier[None], axis=1)
    first_owner = jnp.where(first, owners, -1)
    ranks = jnp.sum(
        ((first_owner[:, :, None] == owners[:, None, :]) & earlier[None]).astype(jnp.int32), axis=1
    )
    rounds = (jnp.max(jnp.where(first, ranks, 0)) + SLOTS) // SLOTS

    local = paired - fsdp_index * vocab_rows
    sent_rank = jnp.where(first_owner == fsdp_index, ranks, -1)
    own_ids = lax.dynamic_index_in_dim(paired, pair, 0, keepdims=False)
    own_first = lax.dynamic_index_in_dim(first, pair, 0, keepdims=False)
    own_ranks = lax.dynamic_index_in_dim(ranks, pair, 0, keepdims=False)
    own_owners = lax.dynamic_index_in_dim(owners, pair, 0, keepdims=False)
    got_rank = jnp.sum(
        jnp.where(
            (own_ids[:, None] == own_ids[None, :]) & own_first[:, None], own_ranks[:, None], 0
        ),
        axis=0,
    )

    def wanted_rows(turn):
        slots = turn * SLOTS + jnp.arange(SLOTS, dtype=jnp.int32)
        wanted = jnp.sum(
            jnp.where(sent_rank[:, :, None] == slots[None, None, :], local[:, :, None], 0), axis=1
        )
        wanted = lax.optimization_barrier(wanted)
        rows = embedding.at[wanted.reshape(-1)].get(mode="promise_in_bounds")
        rows = rows.reshape(PAIRS, SLOTS, 2, HALF).transpose(2, 0, 1, 3)
        return rows.reshape(OWNERS, SLOTS, HALF)

    def exchanged(rows):
        return lax.all_to_all(rows, FSDP, split_axis=0, concat_axis=0)

    def placed_rows(turn, rows):
        slot = got_rank - turn * SLOTS
        inside = (slot >= 0) & (slot < SLOTS)
        spot = jnp.where(inside, own_owners * SLOTS + slot, -1)
        pick = spot[:, None] == jnp.arange(OWNERS * SLOTS, dtype=jnp.int32)[None, :]
        return jnp.dot(
            pick.astype(jnp.bfloat16),
            rows.reshape(OWNERS * SLOTS, HALF),
            preferred_element_type=jnp.float32,
        ).astype(jnp.bfloat16)

    rows = exchanged(wanted_rows(0))
    queries, rollout, rows = lax.optimization_barrier((queries, rollout, rows))
    packed = pack_columns(queries, rollout[:, :1024], rollout[:, 1024:])
    own = placed_rows(0, rows)
    weights = []
    for part in packed:
        part = lax.all_to_all(part, TP, split_axis=0, concat_axis=0)
        part = lax.all_gather(part.reshape(HALF, part.shape[-1]), ("z", "c"))
        weights.append(part.reshape(8 * HALF, part.shape[-1]))
    _, own = lax.while_loop(
        lambda state: state[0] < rounds,
        lambda state: (state[0] + 1, state[1] + placed_rows(state[0], exchanged(wanted_rows(state[0])))),
        (jnp.int32(1), own),
    )

    half = TOKENS // 2
    across = send(own, other_xl)
    below = send(own, along_y(1))
    above = send(own, along_y(-1))
    far_low = send(below[:half], along_y(1))
    far_high = send(above[half:], along_y(-1))
    below_across = send(across, along_y(1))
    above_across = send(across, along_y(-1))
    far_low_across = send(far_low, other_xl)
    far_high_across = send(far_high, other_xl)
    members = [
        y * 2 + xl,
        y * 2 + 1 - xl,
        (y + 3) % 4 * 2 + xl,
        (y + 1) % 4 * 2 + xl,
        (y + 3) % 4 * 2 + 1 - xl,
        (y + 1) % 4 * 2 + 1 - xl,
        (y + 2) % 4 * 2 + xl,
        (y + 2) % 4 * 2 + 1 - xl,
    ]
    place = jnp.stack([member % 4 * 2 + member // 4 for member in members] + [xh]).astype(jnp.int32)
    blocks = (
        own,
        across,
        below,
        above,
        below_across,
        above_across,
        far_low,
        far_high,
        far_low_across,
        far_high_across,
    )
    mine_first, other_first, tokens = project(place, blocks, weights[0])
    came_first = send(other_first, other_xh)
    k_cache, v_cache, _ = lax.optimization_barrier((k_cache, v_cache, other_first))
    k_cache, v_cache = hold(k_cache, v_cache)
    total_second = jnp.dot(tokens, weights[1], preferred_element_type=jnp.float32)
    mine_second = lax.dynamic_slice_in_dim(total_second, xh * half, half, 0)
    other_second = lax.dynamic_slice_in_dim(total_second, (1 - xh) * half, half, 0)
    came_second = send(other_second.astype(jnp.bfloat16), other_xh)

    cosine, sine = rotation(cache_lengths[None, :] + jnp.arange(2, dtype=jnp.int32)[:, None])
    inside = jnp.arange(HEAD, dtype=jnp.int32)[None, :] < cache_lengths[:, None]
    mask = jnp.where(inside, 0.0, -1e30).astype(jnp.float32)
    mask = jnp.broadcast_to(mask[:, None, :], (ROWS, 8, HEAD))
    wide = q_bias.astype(jnp.float32)
    bias_first = jnp.concatenate([wide[:PART], kv_bias.reshape(256).astype(jnp.float32)])

    def stepwise(array):
        return array.reshape(2, ROWS, array.shape[-1])

    context, keys, values, scale = attend(
        True,
        stepwise(mine_first),
        stepwise(came_first),
        bias_first[None],
        cosine,
        sine,
        mask,
        k_cache,
        v_cache,
    )
    context = attend(
        False,
        stepwise(mine_second),
        stepwise(came_second),
        wide[None, PART:],
        cosine,
        sine,
        mask,
        k_cache,
        v_cache,
        keys,
        values,
        scale,
        context,
    )
    return (context, master_new, moment1_new, moment2_new)


def solution(mesh):
    parts = Mesh(mesh.devices.reshape(SIZES), NAMES)
    placed = (
        P(),
        P(FSDP, TP),
        P(FSDP),
        P(NAMES, None),
        P(TP),
        P(None, TP),
        P(NAMES, None, None),
        P(NAMES, None, None),
        P(NAMES, None, None),
        P(NAMES, None, None),
        P(FSDP, None, TP),
        P(FSDP, None, TP),
    )
    return jax.shard_map(
        per_device,
        mesh=parts,
        in_specs=placed,
        out_specs=(
            P(None, FSDP, TP),
            P(NAMES, None, None),
            P(NAMES, None, None),
            P(NAMES, None, None),
        ),
        check_vma=False,
    )
```

```python
import functools
import functools
import math

import jax
import jax.numpy as jnp
from jax import lax
from jax.experimental import pallas as pl
from jax.experimental.pallas import tpu as pltpu
from jax.sharding import Mesh
from jax.sharding import PartitionSpec as P

D = 8192
HEAD = 128
ADAM_STEP = 10

NAMES = ("xh", "z", "c", "y", "xl")
SIZES = (2, 4, 2, 4, 2)
FSDP = ("xh", "z", "c")
TP = ("y", "xl")
OWNERS = 16
PAIRS = 8
ROWS = 160
TOKENS = 4 * ROWS
HALF = 512
SLOTS = 56
PART = 512
FIRST = 768


def pairs_of(move):
    found = []
    total = math.prod(SIZES)
    for index in range(total):
        rest, coords = index, []
        for size in reversed(SIZES):
            coords.append(rest % size)
            rest //= size
        target = 0
        for value, size in zip(move(*reversed(coords)), SIZES):
            target = target * size + value
        found.append((index, target))
    return found


def send(array, move):
    return lax.ppermute(array, NAMES, pairs_of(move))


def along_y(step):
    return lambda xh, z, c, y, xl: (xh, z, c, (y + step) % 4, xl)


def other_xl(xh, z, c, y, xl):
    return (xh, z, c, y, 1 - xl)


def other_xh(xh, z, c, y, xl):
    return (1 - xh, z, c, y, xl)


def swap_xh_core(xh, z, c, y, xl):
    return (c, z, xh, y, xl)


def adamw_update(master, moment1, moment2, gradient):
    gradient = gradient.astype(jnp.float32)
    moment1_new = 0.9 * moment1 + 0.1 * gradient
    moment2_new = 0.95 * moment2 + 0.05 * gradient * gradient
    first_fix = 1.0 - 0.9**ADAM_STEP
    second_fix = 1.0 - 0.95**ADAM_STEP
    update = moment1_new / first_fix / (jnp.sqrt(moment2_new / second_fix) + 1e-08)
    master_new = master - 0.01 * (update + 0.1 * master)
    return (master_new, moment1_new, moment2_new)


def rotation(positions):
    half = HEAD // 2
    freqs = jnp.exp(jnp.arange(half, dtype=jnp.float32) * (-math.log(1000000.0) / half))
    angles = positions[:, :, None].astype(jnp.float32) * freqs
    cosine, sine = jnp.cos(angles), jnp.sin(angles)
    return jnp.concatenate([cosine, cosine], axis=-1), jnp.concatenate([-sine, sine], axis=-1)


def pack_kernel(query_ref, key_ref, value_ref, first_ref, second_ref):
    for member in range(8):
        start = member * 1024
        own = slice(member * 128, member * 128 + 128)
        first_ref[member, :, 0:PART] = query_ref[:, start : start + PART]
        first_ref[member, :, PART : PART + 128] = key_ref[:, own]
        first_ref[member, :, PART + 128 : FIRST] = value_ref[:, own]
        second_ref[member] = query_ref[:, start + PART : start + 1024]


def pack_columns(q_weight, keys, values):
    rows = q_weight.shape[0]
    whole = pl.BlockSpec(memory_space=pltpu.VMEM)
    return pl.pallas_call(
        pack_kernel,
        in_specs=[whole] * 3,
        out_specs=[whole] * 2,
        out_shape=[
            jax.ShapeDtypeStruct((8, rows, FIRST), jnp.bfloat16),
            jax.ShapeDtypeStruct((8, rows, PART), jnp.bfloat16),
        ],
        compiler_params=pltpu.CompilerParams(vmem_limit_bytes=16 << 20),
        cost_estimate=pl.CostEstimate(flops=0, bytes_accessed=3 << 20, transcendentals=0),
    )(q_weight, keys, values)


def project_kernel(place_ref, *refs):
    blocks, w_ref, mine_ref, other_ref, sums_ref, tokens_ref, held, total, sems = (
        refs[:10],
        *refs[10:18],
    )
    half = TOKENS // 2
    width = w_ref.shape[1]
    columns = mine_ref.shape[1] - 128
    keep = pltpu.make_async_copy(held, tokens_ref, sems.at[10])
    step = pl.program_id(0)

    @pl.when(step == 0)
    def _():
        copies = []
        for index in range(10):
            member = index if index < 6 else 6 + (index - 6) // 2
            features = pl.ds(pl.multiple_of(place_ref[member] * HALF, HALF), HALF)
            if index < 6:
                target = held.at[:, features]
            else:
                target = held.at[pl.ds((index - 6) % 2 * half, half), features]
            copies.append(pltpu.make_async_copy(blocks[index], target, sems.at[index]))
        for copy in copies:
            copy.start()
        for copy in copies:
            copy.wait()
        keep.start()

    xh = place_ref[8]
    own = pl.ds(pl.multiple_of(xh * half, half), half)
    partner = pl.ds(pl.multiple_of((1 - xh) * half, half), half)
    tile = pl.ds(pl.multiple_of(step * width, width), width)
    total[...] = jnp.dot(held[...], w_ref[...], preferred_element_type=jnp.float32)
    other_ref[:, tile] = total[partner, :].astype(jnp.bfloat16)
    mine_ref[:, tile] = total[own, :]

    @pl.when(step == 0)
    def _():
        def sums(rows):
            parts = jnp.zeros((half, 128), jnp.float32)
            for start in range(0, 8 * HALF, 128):
                part = held[rows, start : start + 128].astype(jnp.float32)
                parts += part * part
            return jnp.sum(parts, axis=1, keepdims=True)

        mine_ref[:, columns:] = jnp.broadcast_to(sums(own), (half, 128))
        sums_ref[...] = jnp.broadcast_to(sums(partner), (half, 128))

    @pl.when(step == pl.num_programs(0) - 1)
    def _():
        keep.wait()


def project(place, blocks, weights):
    half = TOKENS // 2
    columns = weights.shape[1]
    width = columns + 128
    anywhere = pl.BlockSpec(memory_space=pltpu.HBM)
    return pl.pallas_call(
        project_kernel,
        grid_spec=pltpu.PrefetchScalarGridSpec(
            num_scalar_prefetch=1,
            grid=(columns // 256,),
            in_specs=[anywhere] * 10 + [pl.BlockSpec((8 * HALF, 256), lambda n, place: (0, n))],
            out_specs=[
                pl.BlockSpec((half, width), lambda n, place: (0, 0)),
                pl.BlockSpec((half, columns), lambda n, place: (0, 0)),
                pl.BlockSpec((half, 128), lambda n, place: (0, 0)),
                anywhere,
            ],
            scratch_shapes=[
                pltpu.VMEM((TOKENS, 8 * HALF), jnp.bfloat16),
                pltpu.VMEM((TOKENS, 256), jnp.float32),
                pltpu.SemaphoreType.DMA((11,)),
            ],
        ),
        out_shape=[
            jax.ShapeDtypeStruct((half, width), jnp.float32),
            jax.ShapeDtypeStruct((half, columns), jnp.bfloat16),
            jax.ShapeDtypeStruct((half, 128), jnp.float32),
            jax.ShapeDtypeStruct((TOKENS, 8 * HALF), jnp.bfloat16),
        ],
        compiler_params=pltpu.CompilerParams(vmem_limit_bytes=60 << 20),
        cost_estimate=pl.CostEstimate(
            flops=2 * TOKENS * 4096 * columns, bytes_accessed=12 << 20, transcendentals=0
        ),
    )(place, *blocks, weights)


def hold_kernel(keys, values, keys_out, values_out, sems):
    copies = []
    for index in range(5):
        rows = pl.ds(index * 32, 32)
        copies.append(pltpu.make_async_copy(keys.at[rows], keys_out.at[rows], sems.at[index]))
        copies.append(
            pltpu.make_async_copy(values.at[rows], values_out.at[rows], sems.at[5 + index])
        )
    for copy in copies:
        copy.start()
    for copy in copies:
        copy.wait()


def hold(k_cache, v_cache):
    far = pl.BlockSpec(memory_space=pltpu.HBM)
    near = pl.BlockSpec(memory_space=pltpu.VMEM)
    return pl.pallas_call(
        hold_kernel,
        in_specs=[far, far],
        out_specs=[near, near],
        out_shape=[jax.ShapeDtypeStruct(k_cache.shape, k_cache.dtype)] * 2,
        scratch_shapes=[pltpu.SemaphoreType.DMA((10,))],
        compiler_params=pltpu.CompilerParams(vmem_limit_bytes=12 << 20),
        cost_estimate=pl.CostEstimate(flops=0, bytes_accessed=20 << 20, transcendentals=0),
    )(k_cache, v_cache)


BLOCK = 32


def spread(scratch, array):
    for index in range(8):
        scratch[pl.ds(index, BLOCK, stride=8), :] = array
    return scratch[...].reshape(BLOCK, 8, HEAD)


def attend_kernel(first, *refs):
    if first:
        mine, came, bias, cosine, sine, mask, k_ref, v_ref, came_sums = refs[:9]
        out, keys_out, values_out, scale_out = refs[9:13]
        work = refs[13]
        spare = refs[14:]
    else:
        mine, came, bias, cosine, sine, mask, k_ref, v_ref = refs[:8]
        keys_in, values_in, scale_in = refs[8:11]
        out = refs[12]
        work = refs[13]
        spare = refs[14:]

    def rotated(field, step):
        return field * cosine[step] + pltpu.roll(field, HEAD // 2, 1) * sine[step]

    def raw(step, start, scale):
        features = slice(start, start + HEAD)
        total = mine[step, :, features] + came[step, :, features].astype(jnp.float32)
        return total * scale + bias[:, features]

    new_keys, new_values = [], []
    for step in range(2):
        if first:
            sums = mine[step, :, FIRST : FIRST + 128] + came_sums[step]
            scale = lax.rsqrt(sums / D + 1e-06) / math.sqrt(D)
            scale_out[step] = scale
            key = rotated(raw(step, PART, scale), step).astype(jnp.bfloat16)
            value = raw(step, PART + HEAD, scale).astype(jnp.bfloat16)
            keys_out[step] = key
            values_out[step] = value
        else:
            scale = scale_in[step]
            key, value = keys_in[step], values_in[step]
        new_keys.append(key.astype(jnp.float32))
        new_values.append(value.astype(jnp.float32))
        for head in range(4):
            query = rotated(raw(step, head * HEAD, scale), step)
            work[pl.ds(step * 4 + head, BLOCK, stride=8), :] = query
    queries = work[...].reshape(BLOCK, 8, HEAD).astype(jnp.bfloat16)
    wide = queries.astype(jnp.float32)
    root = 1.0 / math.sqrt(HEAD)
    near = pl.ds(pl.multiple_of(pl.program_id(0) * BLOCK, BLOCK), BLOCK)
    scores = (
        lax.dot_general(
            queries, k_ref[near], (((2,), (2,)), ((0,), (0,))), preferred_element_type=jnp.float32
        )
        * root
        + mask[...]
    )
    second = lax.broadcasted_iota(jnp.int32, (BLOCK, 8, 1), 1) >= 4
    own = [
        jnp.sum(wide * spread(spare[u], new_keys[u]), axis=2, keepdims=True) * root
        for u in range(2)
    ]
    own[1] = jnp.where(second, own[1], -1e30)
    peak = jnp.maximum(
        jnp.max(scores, axis=2, keepdims=True), jnp.maximum(own[0], own[1])
    )
    shares = jnp.exp(scores - peak)
    own = [jnp.exp(score - peak) for score in own]
    total = jnp.sum(shares, axis=2, keepdims=True) + own[0] + own[1]
    inverse = 1.0 / total
    weights = (shares * inverse).astype(jnp.bfloat16)
    context = lax.dot_general(
        weights, v_ref[near], (((2,), (1,)), ((0,), (0,))), preferred_element_type=jnp.float32
    )
    for u in range(2):
        weight = (own[u] * inverse).astype(jnp.bfloat16).astype(jnp.float32)
        context += weight * spread(spare[2 + u], new_values[u])
    work[...] = context.reshape(BLOCK * 8, HEAD)
    for step in range(2):
        for head in range(4):
            result = work[pl.ds(step * 4 + head, BLOCK, stride=8), :]
            out[step, :, head * HEAD : (head + 1) * HEAD] = result.astype(jnp.bfloat16)


def attend(first, mine, came, bias, cosine, sine, mask, k_cache, v_cache, *more):
    width = mine.shape[-1]

    def steps(columns):
        return pl.BlockSpec((2, BLOCK, columns), lambda i: (0, i, 0))

    def rows(a, b):
        return pl.BlockSpec((BLOCK, a, b), lambda i: (i, 0, 0))

    in_specs = [
        steps(width),
        steps(came.shape[-1]),
        pl.BlockSpec((1, bias.shape[-1]), lambda i: (0, 0)),
        steps(HEAD),
        steps(HEAD),
        rows(8, HEAD),
        pl.BlockSpec(memory_space=pltpu.VMEM),
        pl.BlockSpec(memory_space=pltpu.VMEM),
    ]
    context = jax.ShapeDtypeStruct((2, ROWS, 2 * PART), jnp.bfloat16)
    if first:
        in_specs += [steps(HEAD)]
        out_specs = [steps(PART), steps(HEAD), steps(HEAD), steps(HEAD)]
        out_shape = [
            context,
            jax.ShapeDtypeStruct((2, ROWS, HEAD), jnp.bfloat16),
            jax.ShapeDtypeStruct((2, ROWS, HEAD), jnp.bfloat16),
            jax.ShapeDtypeStruct((2, ROWS, HEAD), jnp.float32),
        ]
        aliases = {}
    else:
        in_specs += [steps(HEAD), steps(HEAD), steps(HEAD), pl.BlockSpec(memory_space=pl.ANY)]
        out_specs = pl.BlockSpec((2, BLOCK, PART), lambda i: (0, i, 1))
        out_shape = context
        aliases = {11: 0}
    return pl.pallas_call(
        functools.partial(attend_kernel, first),
        grid=(ROWS // BLOCK,),
        in_specs=in_specs,
        out_specs=out_specs,
        out_shape=out_shape,
        scratch_shapes=[pltpu.VMEM((BLOCK * 8, HEAD), jnp.float32)] * 5,
        input_output_aliases=aliases,
        compiler_params=pltpu.CompilerParams(vmem_limit_bytes=24 << 20),
        cost_estimate=pl.CostEstimate(
            flops=4 * ROWS * 8 * 128 * 128, bytes_accessed=12 << 20, transcendentals=ROWS * 1024
        ),
    )(mine, came, bias, cosine, sine, mask, k_cache, v_cache, *more)


def per_device(
    token_ids,
    embedding,
    cache_lengths,
    q_weight,
    q_bias,
    kv_bias,
    kv_master,
    kv_moment1,
    kv_moment2,
    kv_grad,
    k_cache,
    v_cache,
):
    xh, z, c = (lax.axis_index(name) for name in FSDP)
    y, xl = (lax.axis_index(name) for name in TP)
    fsdp_index = (xh * 4 + z) * 2 + c
    pair = z * 2 + c
    vocab_rows = embedding.shape[0]

    queries = send(q_weight, swap_xh_core)
    master_new, moment1_new, moment2_new = adamw_update(kv_master, kv_moment1, kv_moment2, kv_grad)
    rollout = master_new.astype(jnp.bfloat16)
    rollout = jnp.concatenate([rollout[:, 0, :], rollout[:, 1, :]], axis=1)
    rollout = send(rollout, swap_xh_core)

    paired = token_ids.reshape(2, 2, PAIRS, ROWS).transpose(2, 1, 0, 3).reshape(PAIRS, TOKENS)
    owners = paired // vocab_rows
    order = jnp.arange(TOKENS, dtype=jnp.int32)
    earlier = order[:, None] < order[None, :]
    same_id = paired[:, :, None] == paired[:, None, :]
    first = ~jnp.any(same_id & earlier[None], axis=1)
    counts = jnp.sum(
        (first[:, None, :] & (owners[:, None, :] == jnp.arange(OWNERS)[None, :, None])).astype(
            jnp.int32
        ),
        axis=2,
    )
    rounds = (jnp.max(counts) + SLOTS - 1) // SLOTS

    def ranks_in(chosen):
        return jnp.dot(
            chosen.astype(jnp.bfloat16),
            earlier.astype(jnp.bfloat16),
            preferred_element_type=jnp.float32,
        ).astype(jnp.int32)

    local = paired - fsdp_index * vocab_rows
    sent = first & (owners == fsdp_index)
    sent_rank = jnp.where(sent, ranks_in(sent), -1)
    own_ids = lax.dynamic_index_in_dim(paired, pair, 0, keepdims=False)
    own_first = lax.dynamic_index_in_dim(first, pair, 0, keepdims=False)
    own_owners = lax.dynamic_index_in_dim(owners, pair, 0, keepdims=False)
    by_owner = own_first[None, :] & (own_owners[None, :] == jnp.arange(OWNERS)[:, None])
    own_ranks = jnp.sum(jnp.where(by_owner, ranks_in(by_owner), 0), axis=0)
    got_rank = jnp.sum(
        jnp.where(
            (own_ids[:, None] == own_ids[None, :]) & own_first[:, None], own_ranks[:, None], 0
        ),
        axis=0,
    )

    def wanted_rows(turn):
        slots = turn * SLOTS + jnp.arange(SLOTS, dtype=jnp.int32)
        wanted = jnp.sum(
            jnp.where(sent_rank[:, :, None] == slots[None, None, :], local[:, :, None], 0), axis=1
        )
        wanted = lax.optimization_barrier(wanted)
        rows = embedding.at[wanted.reshape(-1)].get(mode="promise_in_bounds")
        rows = rows.reshape(PAIRS, SLOTS, 2, HALF).transpose(2, 0, 1, 3)
        return rows.reshape(OWNERS, SLOTS, HALF)

    def exchanged(rows):
        return lax.all_to_all(rows, FSDP, split_axis=0, concat_axis=0)

    def placed_rows(turn, rows):
        slot = got_rank - turn * SLOTS
        inside = (slot >= 0) & (slot < SLOTS)
        spot = jnp.where(inside, own_owners * SLOTS + slot, -1)
        pick = spot[:, None] == jnp.arange(OWNERS * SLOTS, dtype=jnp.int32)[None, :]
        return jnp.dot(
            pick.astype(jnp.bfloat16),
            rows.reshape(OWNERS * SLOTS, HALF),
            preferred_element_type=jnp.float32,
        ).astype(jnp.bfloat16)

    rows = exchanged(wanted_rows(0))
    queries, rollout, rows = lax.optimization_barrier((queries, rollout, rows))
    first_part, second_part = pack_columns(queries, rollout[:, :1024], rollout[:, 1024:])

    def gathered(part):
        part = lax.all_to_all(part, TP, split_axis=0, concat_axis=0)
        part = lax.all_gather(part.reshape(HALF, part.shape[-1]), ("z", "c"))
        return part.reshape(8 * HALF, part.shape[-1])

    weights = [gathered(first_part), gathered(second_part)]
    own = placed_rows(0, rows)
    _, own = lax.while_loop(
        lambda state: state[0] < rounds,
        lambda state: (state[0] + 1, state[1] + placed_rows(state[0], exchanged(wanted_rows(state[0])))),
        (jnp.int32(1), own),
    )

    half = TOKENS // 2
    across = send(own, other_xl)
    below = send(own, along_y(1))
    above = send(own, along_y(-1))
    far_low = send(below[:half], along_y(1))
    far_high = send(above[half:], along_y(-1))
    below_across = send(across, along_y(1))
    above_across = send(across, along_y(-1))
    far_low_across = send(far_low, other_xl)
    far_high_across = send(far_high, other_xl)
    members = [
        y * 2 + xl,
        y * 2 + 1 - xl,
        (y + 3) % 4 * 2 + xl,
        (y + 1) % 4 * 2 + xl,
        (y + 3) % 4 * 2 + 1 - xl,
        (y + 1) % 4 * 2 + 1 - xl,
        (y + 2) % 4 * 2 + xl,
        (y + 2) % 4 * 2 + 1 - xl,
    ]
    place = jnp.stack([member % 4 * 2 + member // 4 for member in members] + [xh]).astype(jnp.int32)
    blocks = (
        own,
        across,
        below,
        above,
        below_across,
        above_across,
        far_low,
        far_high,
        far_low_across,
        far_high_across,
    )
    mine_first, other_first, other_sums, tokens = project(place, blocks, weights[0])
    came_first = send(other_first, other_xh)
    came_sums = send(other_sums[:, 0], other_xh)
    came_sums = jnp.broadcast_to(came_sums[:, None], (half, HEAD))
    k_cache, v_cache, _ = lax.optimization_barrier((k_cache, v_cache, other_first))
    k_cache, v_cache = hold(k_cache, v_cache)
    total_second = jnp.dot(tokens, weights[1], preferred_element_type=jnp.float32)
    mine_second = lax.dynamic_slice_in_dim(total_second, xh * half, half, 0)
    other_second = lax.dynamic_slice_in_dim(total_second, (1 - xh) * half, half, 0)
    came_second = send(other_second.astype(jnp.bfloat16), other_xh)

    cosine, sine = rotation(cache_lengths[None, :] + jnp.arange(2, dtype=jnp.int32)[:, None])
    inside = jnp.arange(HEAD, dtype=jnp.int32)[None, :] < cache_lengths[:, None]
    mask = jnp.where(inside, 0.0, -1e30).astype(jnp.float32)
    mask = jnp.broadcast_to(mask[:, None, :], (ROWS, 8, HEAD))
    wide = q_bias.astype(jnp.float32)
    bias_first = jnp.concatenate([wide[:PART], kv_bias.reshape(256).astype(jnp.float32)])

    def stepwise(array):
        return array.reshape(2, ROWS, array.shape[-1])

    context, keys, values, scale = attend(
        True,
        stepwise(mine_first),
        stepwise(came_first),
        bias_first[None],
        cosine,
        sine,
        mask,
        k_cache,
        v_cache,
        stepwise(came_sums),
    )
    context = attend(
        False,
        stepwise(mine_second),
        stepwise(came_second),
        wide[None, PART:],
        cosine,
        sine,
        mask,
        k_cache,
        v_cache,
        keys,
        values,
        scale,
        context,
    )
    return (context, master_new, moment1_new, moment2_new)


def solution(mesh):
    parts = Mesh(mesh.devices.reshape(SIZES), NAMES)
    placed = (
        P(),
        P(FSDP, TP),
        P(FSDP),
        P(NAMES, None),
        P(TP),
        P(None, TP),
        P(NAMES, None, None),
        P(NAMES, None, None),
        P(NAMES, None, None),
        P(NAMES, None, None),
        P(FSDP, None, TP),
        P(FSDP, None, TP),
    )
    return jax.shard_map(
        per_device,
        mesh=parts,
        in_specs=placed,
        out_specs=(
            P(None, FSDP, TP),
            P(NAMES, None, None),
            P(NAMES, None, None),
            P(NAMES, None, None),
        ),
        check_vma=False,
    )
```

```python
import functools
import functools
import math

import jax
import jax.numpy as jnp
from jax import lax
from jax.experimental import pallas as pl
from jax.experimental.pallas import tpu as pltpu
from jax.sharding import Mesh
from jax.sharding import PartitionSpec as P

D = 8192
HEAD = 128
ADAM_STEP = 10

NAMES = ("xh", "z", "c", "y", "xl")
SIZES = (2, 4, 2, 4, 2)
FSDP = ("xh", "z", "c")
TP = ("y", "xl")
OWNERS = 16
PAIRS = 8
ROWS = 160
TOKENS = 4 * ROWS
HALF = 512
SLOTS = 56
PART = 512
FIRST = 768


def pairs_of(move):
    found = []
    total = math.prod(SIZES)
    for index in range(total):
        rest, coords = index, []
        for size in reversed(SIZES):
            coords.append(rest % size)
            rest //= size
        target = 0
        for value, size in zip(move(*reversed(coords)), SIZES):
            target = target * size + value
        found.append((index, target))
    return found


def send(array, move):
    return lax.ppermute(array, NAMES, pairs_of(move))


def along_y(step):
    return lambda xh, z, c, y, xl: (xh, z, c, (y + step) % 4, xl)


def other_xl(xh, z, c, y, xl):
    return (xh, z, c, y, 1 - xl)


def other_xh(xh, z, c, y, xl):
    return (1 - xh, z, c, y, xl)


def swap_xh_core(xh, z, c, y, xl):
    return (c, z, xh, y, xl)


def adamw_update(master, moment1, moment2, gradient):
    gradient = gradient.astype(jnp.float32)
    moment1_new = 0.9 * moment1 + 0.1 * gradient
    moment2_new = 0.95 * moment2 + 0.05 * gradient * gradient
    first_fix = 1.0 - 0.9**ADAM_STEP
    second_fix = 1.0 - 0.95**ADAM_STEP
    update = moment1_new / first_fix / (jnp.sqrt(moment2_new / second_fix) + 1e-08)
    master_new = master - 0.01 * (update + 0.1 * master)
    return (master_new, moment1_new, moment2_new)


def rotation(positions):
    half = HEAD // 2
    freqs = jnp.exp(jnp.arange(half, dtype=jnp.float32) * (-math.log(1000000.0) / half))
    angles = positions[:, :, None].astype(jnp.float32) * freqs
    cosine, sine = jnp.cos(angles), jnp.sin(angles)
    return jnp.concatenate([cosine, cosine], axis=-1), jnp.concatenate([-sine, sine], axis=-1)


def pack_kernel(query_ref, key_ref, value_ref, first_ref, second_ref):
    for member in range(8):
        start = member * 1024
        own = slice(member * 128, member * 128 + 128)
        first_ref[member, :, 0:PART] = query_ref[:, start : start + PART]
        first_ref[member, :, PART : PART + 128] = key_ref[:, own]
        first_ref[member, :, PART + 128 : FIRST] = value_ref[:, own]
        second_ref[member] = query_ref[:, start + PART : start + 1024]


def pack_columns(q_weight, keys, values):
    rows = q_weight.shape[0]
    whole = pl.BlockSpec(memory_space=pltpu.VMEM)
    return pl.pallas_call(
        pack_kernel,
        in_specs=[whole] * 3,
        out_specs=[whole] * 2,
        out_shape=[
            jax.ShapeDtypeStruct((8, rows, FIRST), jnp.bfloat16),
            jax.ShapeDtypeStruct((8, rows, PART), jnp.bfloat16),
        ],
        compiler_params=pltpu.CompilerParams(vmem_limit_bytes=16 << 20),
        cost_estimate=pl.CostEstimate(flops=0, bytes_accessed=3 << 20, transcendentals=0),
    )(q_weight, keys, values)


def project_kernel(place_ref, *refs):
    blocks, w_ref, mine_ref, other_ref, tokens_ref, held, total, sems = refs[:10], *refs[10:17]
    half = TOKENS // 2
    width = w_ref.shape[1]
    columns = mine_ref.shape[1] - 128
    keep = pltpu.make_async_copy(held, tokens_ref, sems.at[10])
    step = pl.program_id(0)

    @pl.when(step == 0)
    def _():
        copies = []
        for index in range(10):
            member = index if index < 6 else 6 + (index - 6) // 2
            features = pl.ds(pl.multiple_of(place_ref[member] * HALF, HALF), HALF)
            if index < 6:
                target = held.at[:, features]
            else:
                target = held.at[pl.ds((index - 6) % 2 * half, half), features]
            copies.append(pltpu.make_async_copy(blocks[index], target, sems.at[index]))
        for copy in copies:
            copy.start()
        for copy in copies:
            copy.wait()
        keep.start()

    xh = place_ref[8]
    own = pl.ds(pl.multiple_of(xh * half, half), half)
    partner = pl.ds(pl.multiple_of((1 - xh) * half, half), half)
    tile = pl.ds(pl.multiple_of(step * width, width), width)
    total[...] = jnp.dot(held[...], w_ref[...], preferred_element_type=jnp.float32)
    other_ref[:, tile] = total[partner, :].astype(jnp.bfloat16)
    mine_ref[:, tile] = total[own, :]

    @pl.when(step == 0)
    def _():
        def sums(rows):
            parts = jnp.zeros((half, 128), jnp.float32)
            for start in range(0, 8 * HALF, 128):
                part = held[rows, start : start + 128].astype(jnp.float32)
                parts += part * part
            return jnp.sum(parts, axis=1, keepdims=True)

        mine_ref[:, columns:] = jnp.broadcast_to(sums(own), (half, 128))
        partner_sums = sums(partner)
        high = partner_sums.astype(jnp.bfloat16).astype(jnp.float32)
        lanes = lax.broadcasted_iota(jnp.int32, (half, 128), 1)
        other_ref[:, columns:] = jnp.where(lanes < 64, high, partner_sums - high).astype(
            jnp.bfloat16
        )

    @pl.when(step == pl.num_programs(0) - 1)
    def _():
        keep.wait()


def project(place, blocks, weights):
    half = TOKENS // 2
    columns = weights.shape[1]
    width = columns + 128
    anywhere = pl.BlockSpec(memory_space=pltpu.HBM)
    return pl.pallas_call(
        project_kernel,
        grid_spec=pltpu.PrefetchScalarGridSpec(
            num_scalar_prefetch=1,
            grid=(columns // 256,),
            in_specs=[anywhere] * 10 + [pl.BlockSpec((8 * HALF, 256), lambda n, place: (0, n))],
            out_specs=[
                pl.BlockSpec((half, width), lambda n, place: (0, 0)),
                pl.BlockSpec((half, width), lambda n, place: (0, 0)),
                anywhere,
            ],
            scratch_shapes=[
                pltpu.VMEM((TOKENS, 8 * HALF), jnp.bfloat16),
                pltpu.VMEM((TOKENS, 256), jnp.float32),
                pltpu.SemaphoreType.DMA((11,)),
            ],
        ),
        out_shape=[
            jax.ShapeDtypeStruct((half, width), jnp.float32),
            jax.ShapeDtypeStruct((half, width), jnp.bfloat16),
            jax.ShapeDtypeStruct((TOKENS, 8 * HALF), jnp.bfloat16),
        ],
        compiler_params=pltpu.CompilerParams(vmem_limit_bytes=60 << 20),
        cost_estimate=pl.CostEstimate(
            flops=2 * TOKENS * 4096 * columns, bytes_accessed=12 << 20, transcendentals=0
        ),
    )(place, *blocks, weights)


def hold_kernel(keys, values, keys_out, values_out, sems):
    copies = []
    for index in range(5):
        rows = pl.ds(index * 32, 32)
        copies.append(pltpu.make_async_copy(keys.at[rows], keys_out.at[rows], sems.at[index]))
        copies.append(
            pltpu.make_async_copy(values.at[rows], values_out.at[rows], sems.at[5 + index])
        )
    for copy in copies:
        copy.start()
    for copy in copies:
        copy.wait()


def hold(k_cache, v_cache):
    far = pl.BlockSpec(memory_space=pltpu.HBM)
    near = pl.BlockSpec(memory_space=pltpu.VMEM)
    return pl.pallas_call(
        hold_kernel,
        in_specs=[far, far],
        out_specs=[near, near],
        out_shape=[jax.ShapeDtypeStruct(k_cache.shape, k_cache.dtype)] * 2,
        scratch_shapes=[pltpu.SemaphoreType.DMA((10,))],
        compiler_params=pltpu.CompilerParams(vmem_limit_bytes=12 << 20),
        cost_estimate=pl.CostEstimate(flops=0, bytes_accessed=20 << 20, transcendentals=0),
    )(k_cache, v_cache)


BLOCK = 32


def spread(scratch, array):
    for index in range(8):
        scratch[pl.ds(index, BLOCK, stride=8), :] = array
    return scratch[...].reshape(BLOCK, 8, HEAD)


def attend_kernel(first, *refs):
    if first:
        mine, came, bias, cosine, sine, mask, k_ref, v_ref = refs[:8]
        out, keys_out, values_out, scale_out = refs[8:12]
        work = refs[12]
        spare = refs[13:]
    else:
        mine, came, bias, cosine, sine, mask, k_ref, v_ref = refs[:8]
        keys_in, values_in, scale_in = refs[8:11]
        out = refs[12]
        work = refs[13]
        spare = refs[14:]

    def rotated(field, step):
        return field * cosine[step] + pltpu.roll(field, HEAD // 2, 1) * sine[step]

    def raw(step, start, scale):
        features = slice(start, start + HEAD)
        total = mine[step, :, features] + came[step, :, features].astype(jnp.float32)
        return total * scale + bias[:, features]

    new_keys, new_values = [], []
    for step in range(2):
        if first:
            part = came[step, :, FIRST : FIRST + 128].astype(jnp.float32)
            sums = mine[step, :, FIRST : FIRST + 128] + part + pltpu.roll(part, 64, 1)
            scale = lax.rsqrt(sums / D + 1e-06) / math.sqrt(D)
            scale_out[step] = scale
            key = rotated(raw(step, PART, scale), step).astype(jnp.bfloat16)
            value = raw(step, PART + HEAD, scale).astype(jnp.bfloat16)
            keys_out[step] = key
            values_out[step] = value
        else:
            scale = scale_in[step]
            key, value = keys_in[step], values_in[step]
        new_keys.append(key.astype(jnp.float32))
        new_values.append(value.astype(jnp.float32))
        for head in range(4):
            query = rotated(raw(step, head * HEAD, scale), step)
            work[pl.ds(step * 4 + head, BLOCK, stride=8), :] = query
    queries = work[...].reshape(BLOCK, 8, HEAD).astype(jnp.bfloat16)
    wide = queries.astype(jnp.float32)
    root = 1.0 / math.sqrt(HEAD)
    near = pl.ds(pl.multiple_of(pl.program_id(0) * BLOCK, BLOCK), BLOCK)
    scores = (
        lax.dot_general(
            queries, k_ref[near], (((2,), (2,)), ((0,), (0,))), preferred_element_type=jnp.float32
        )
        * root
        + mask[...]
    )
    second = lax.broadcasted_iota(jnp.int32, (BLOCK, 8, 1), 1) >= 4
    own = [
        jnp.sum(wide * spread(spare[u], new_keys[u]), axis=2, keepdims=True) * root
        for u in range(2)
    ]
    own[1] = jnp.where(second, own[1], -1e30)
    peak = jnp.maximum(
        jnp.max(scores, axis=2, keepdims=True), jnp.maximum(own[0], own[1])
    )
    shares = jnp.exp(scores - peak)
    own = [jnp.exp(score - peak) for score in own]
    total = jnp.sum(shares, axis=2, keepdims=True) + own[0] + own[1]
    inverse = 1.0 / total
    weights = (shares * inverse).astype(jnp.bfloat16)
    context = lax.dot_general(
        weights, v_ref[near], (((2,), (1,)), ((0,), (0,))), preferred_element_type=jnp.float32
    )
    for u in range(2):
        weight = (own[u] * inverse).astype(jnp.bfloat16).astype(jnp.float32)
        context += weight * spread(spare[2 + u], new_values[u])
    work[...] = context.reshape(BLOCK * 8, HEAD)
    for step in range(2):
        for head in range(4):
            result = work[pl.ds(step * 4 + head, BLOCK, stride=8), :]
            out[step, :, head * HEAD : (head + 1) * HEAD] = result.astype(jnp.bfloat16)


def attend(first, mine, came, bias, cosine, sine, mask, k_cache, v_cache, *more):
    width = mine.shape[-1]

    def steps(columns):
        return pl.BlockSpec((2, BLOCK, columns), lambda i: (0, i, 0))

    def rows(a, b):
        return pl.BlockSpec((BLOCK, a, b), lambda i: (i, 0, 0))

    in_specs = [
        steps(width),
        steps(width),
        pl.BlockSpec((1, bias.shape[-1]), lambda i: (0, 0)),
        steps(HEAD),
        steps(HEAD),
        rows(8, HEAD),
        pl.BlockSpec(memory_space=pltpu.VMEM),
        pl.BlockSpec(memory_space=pltpu.VMEM),
    ]
    context = jax.ShapeDtypeStruct((2, ROWS, 2 * PART), jnp.bfloat16)
    if first:
        out_specs = [steps(PART), steps(HEAD), steps(HEAD), steps(HEAD)]
        out_shape = [
            context,
            jax.ShapeDtypeStruct((2, ROWS, HEAD), jnp.bfloat16),
            jax.ShapeDtypeStruct((2, ROWS, HEAD), jnp.bfloat16),
            jax.ShapeDtypeStruct((2, ROWS, HEAD), jnp.float32),
        ]
        aliases = {}
    else:
        in_specs += [steps(HEAD), steps(HEAD), steps(HEAD), pl.BlockSpec(memory_space=pl.ANY)]
        out_specs = pl.BlockSpec((2, BLOCK, PART), lambda i: (0, i, 1))
        out_shape = context
        aliases = {11: 0}
    return pl.pallas_call(
        functools.partial(attend_kernel, first),
        grid=(ROWS // BLOCK,),
        in_specs=in_specs,
        out_specs=out_specs,
        out_shape=out_shape,
        scratch_shapes=[pltpu.VMEM((BLOCK * 8, HEAD), jnp.float32)] * 5,
        input_output_aliases=aliases,
        compiler_params=pltpu.CompilerParams(vmem_limit_bytes=24 << 20),
        cost_estimate=pl.CostEstimate(
            flops=4 * ROWS * 8 * 128 * 128, bytes_accessed=12 << 20, transcendentals=ROWS * 1024
        ),
    )(mine, came, bias, cosine, sine, mask, k_cache, v_cache, *more)


def per_device(
    token_ids,
    embedding,
    cache_lengths,
    q_weight,
    q_bias,
    kv_bias,
    kv_master,
    kv_moment1,
    kv_moment2,
    kv_grad,
    k_cache,
    v_cache,
):
    xh, z, c = (lax.axis_index(name) for name in FSDP)
    y, xl = (lax.axis_index(name) for name in TP)
    fsdp_index = (xh * 4 + z) * 2 + c
    pair = z * 2 + c
    vocab_rows = embedding.shape[0]

    queries = send(q_weight, swap_xh_core)
    master_new, moment1_new, moment2_new = adamw_update(kv_master, kv_moment1, kv_moment2, kv_grad)
    rollout = master_new.astype(jnp.bfloat16)
    rollout = jnp.concatenate([rollout[:, 0, :], rollout[:, 1, :]], axis=1)
    rollout = send(rollout, swap_xh_core)

    paired = token_ids.reshape(2, 2, PAIRS, ROWS).transpose(2, 1, 0, 3).reshape(PAIRS, TOKENS)
    owners = paired // vocab_rows
    order = jnp.arange(TOKENS, dtype=jnp.int32)
    earlier = order[:, None] < order[None, :]
    same_id = paired[:, :, None] == paired[:, None, :]
    first = ~jnp.any(same_id & earlier[None], axis=1)
    counts = jnp.sum(
        (first[:, None, :] & (owners[:, None, :] == jnp.arange(OWNERS)[None, :, None])).astype(
            jnp.int32
        ),
        axis=2,
    )
    rounds = (jnp.max(counts) + SLOTS - 1) // SLOTS

    def ranks_in(chosen):
        return jnp.dot(
            chosen.astype(jnp.bfloat16),
            earlier.astype(jnp.bfloat16),
            preferred_element_type=jnp.float32,
        ).astype(jnp.int32)

    local = paired - fsdp_index * vocab_rows
    sent = first & (owners == fsdp_index)
    sent_rank = jnp.where(sent, ranks_in(sent), -1)
    own_ids = lax.dynamic_index_in_dim(paired, pair, 0, keepdims=False)
    own_first = lax.dynamic_index_in_dim(first, pair, 0, keepdims=False)
    own_owners = lax.dynamic_index_in_dim(owners, pair, 0, keepdims=False)
    by_owner = own_first[None, :] & (own_owners[None, :] == jnp.arange(OWNERS)[:, None])
    own_ranks = jnp.sum(jnp.where(by_owner, ranks_in(by_owner), 0), axis=0)
    got_rank = jnp.sum(
        jnp.where(
            (own_ids[:, None] == own_ids[None, :]) & own_first[:, None], own_ranks[:, None], 0
        ),
        axis=0,
    )

    def wanted_rows(turn):
        slots = turn * SLOTS + jnp.arange(SLOTS, dtype=jnp.int32)
        wanted = jnp.sum(
            jnp.where(sent_rank[:, :, None] == slots[None, None, :], local[:, :, None], 0), axis=1
        )
        wanted = lax.optimization_barrier(wanted)
        rows = embedding.at[wanted.reshape(-1)].get(mode="promise_in_bounds")
        rows = rows.reshape(PAIRS, SLOTS, 2, HALF).transpose(2, 0, 1, 3)
        return rows.reshape(OWNERS, SLOTS, HALF)

    def exchanged(rows):
        return lax.all_to_all(rows, FSDP, split_axis=0, concat_axis=0)

    def placed_rows(turn, rows):
        slot = got_rank - turn * SLOTS
        inside = (slot >= 0) & (slot < SLOTS)
        spot = jnp.where(inside, own_owners * SLOTS + slot, -1)
        pick = spot[:, None] == jnp.arange(OWNERS * SLOTS, dtype=jnp.int32)[None, :]
        return jnp.dot(
            pick.astype(jnp.bfloat16),
            rows.reshape(OWNERS * SLOTS, HALF),
            preferred_element_type=jnp.float32,
        ).astype(jnp.bfloat16)

    rows = exchanged(wanted_rows(0))
    queries, rollout, rows = lax.optimization_barrier((queries, rollout, rows))
    first_part, second_part = pack_columns(queries, rollout[:, :1024], rollout[:, 1024:])

    def gathered(part):
        part = lax.all_to_all(part, TP, split_axis=0, concat_axis=0)
        part = lax.all_gather(part.reshape(HALF, part.shape[-1]), ("z", "c"))
        return part.reshape(8 * HALF, part.shape[-1])

    weights = [gathered(first_part), gathered(second_part)]
    own = placed_rows(0, rows)
    _, own = lax.while_loop(
        lambda state: state[0] < rounds,
        lambda state: (state[0] + 1, state[1] + placed_rows(state[0], exchanged(wanted_rows(state[0])))),
        (jnp.int32(1), own),
    )

    half = TOKENS // 2
    across = send(own, other_xl)
    below = send(own, along_y(1))
    above = send(own, along_y(-1))
    far_low = send(below[:half], along_y(1))
    far_high = send(above[half:], along_y(-1))
    below_across = send(across, along_y(1))
    above_across = send(across, along_y(-1))
    far_low_across = send(far_low, other_xl)
    far_high_across = send(far_high, other_xl)
    members = [
        y * 2 + xl,
        y * 2 + 1 - xl,
        (y + 3) % 4 * 2 + xl,
        (y + 1) % 4 * 2 + xl,
        (y + 3) % 4 * 2 + 1 - xl,
        (y + 1) % 4 * 2 + 1 - xl,
        (y + 2) % 4 * 2 + xl,
        (y + 2) % 4 * 2 + 1 - xl,
    ]
    place = jnp.stack([member % 4 * 2 + member // 4 for member in members] + [xh]).astype(jnp.int32)
    blocks = (
        own,
        across,
        below,
        above,
        below_across,
        above_across,
        far_low,
        far_high,
        far_low_across,
        far_high_across,
    )
    mine_first, other_first, tokens = project(place, blocks, weights[0])
    came_first = send(other_first, other_xh)
    k_cache, v_cache, _ = lax.optimization_barrier((k_cache, v_cache, other_first))
    k_cache, v_cache = hold(k_cache, v_cache)
    total_second = jnp.dot(tokens, weights[1], preferred_element_type=jnp.float32)
    mine_second = lax.dynamic_slice_in_dim(total_second, xh * half, half, 0)
    other_second = lax.dynamic_slice_in_dim(total_second, (1 - xh) * half, half, 0)
    came_second = send(other_second.astype(jnp.bfloat16), other_xh)

    cosine, sine = rotation(cache_lengths[None, :] + jnp.arange(2, dtype=jnp.int32)[:, None])
    inside = jnp.arange(HEAD, dtype=jnp.int32)[None, :] < cache_lengths[:, None]
    mask = jnp.where(inside, 0.0, -1e30).astype(jnp.float32)
    mask = jnp.broadcast_to(mask[:, None, :], (ROWS, 8, HEAD))
    wide = q_bias.astype(jnp.float32)
    bias_first = jnp.concatenate([wide[:PART], kv_bias.reshape(256).astype(jnp.float32)])

    def stepwise(array):
        return array.reshape(2, ROWS, array.shape[-1])

    context, keys, values, scale = attend(
        True,
        stepwise(mine_first),
        stepwise(came_first),
        bias_first[None],
        cosine,
        sine,
        mask,
        k_cache,
        v_cache,
    )
    context = attend(
        False,
        stepwise(mine_second),
        stepwise(came_second),
        wide[None, PART:],
        cosine,
        sine,
        mask,
        k_cache,
        v_cache,
        keys,
        values,
        scale,
        context,
    )
    return (context, master_new, moment1_new, moment2_new)


def solution(mesh):
    parts = Mesh(mesh.devices.reshape(SIZES), NAMES)
    placed = (
        P(),
        P(FSDP, TP),
        P(FSDP),
        P(NAMES, None),
        P(TP),
        P(None, TP),
        P(NAMES, None, None),
        P(NAMES, None, None),
        P(NAMES, None, None),
        P(NAMES, None, None),
        P(FSDP, None, TP),
        P(FSDP, None, TP),
    )
    return jax.shard_map(
        per_device,
        mesh=parts,
        in_specs=placed,
        out_specs=(
            P(None, FSDP, TP),
            P(NAMES, None, None),
            P(NAMES, None, None),
            P(NAMES, None, None),
        ),
        check_vma=False,
    )
```

```python
import functools
import functools
import math

import jax
import jax.numpy as jnp
from jax import lax
from jax.experimental import pallas as pl
from jax.experimental.pallas import tpu as pltpu
from jax.sharding import Mesh
from jax.sharding import PartitionSpec as P

D = 8192
HEAD = 128
ADAM_STEP = 10

NAMES = ("xh", "z", "c", "y", "xl")
SIZES = (2, 4, 2, 4, 2)
FSDP = ("xh", "z", "c")
TP = ("y", "xl")
OWNERS = 16
PAIRS = 8
ROWS = 160
TOKENS = 4 * ROWS
HALF = 512
SLOTS = 56
PART = 512
FIRST = 768


def pairs_of(move):
    found = []
    total = math.prod(SIZES)
    for index in range(total):
        rest, coords = index, []
        for size in reversed(SIZES):
            coords.append(rest % size)
            rest //= size
        target = 0
        for value, size in zip(move(*reversed(coords)), SIZES):
            target = target * size + value
        found.append((index, target))
    return found


def send(array, move):
    return lax.ppermute(array, NAMES, pairs_of(move))


def along_y(step):
    return lambda xh, z, c, y, xl: (xh, z, c, (y + step) % 4, xl)


def other_xl(xh, z, c, y, xl):
    return (xh, z, c, y, 1 - xl)


def other_xh(xh, z, c, y, xl):
    return (1 - xh, z, c, y, xl)


def swap_xh_core(xh, z, c, y, xl):
    return (c, z, xh, y, xl)


def adamw_update(master, moment1, moment2, gradient):
    gradient = gradient.astype(jnp.float32)
    moment1_new = 0.9 * moment1 + 0.1 * gradient
    moment2_new = 0.95 * moment2 + 0.05 * gradient * gradient
    first_fix = 1.0 - 0.9**ADAM_STEP
    second_fix = 1.0 - 0.95**ADAM_STEP
    update = moment1_new / first_fix / (jnp.sqrt(moment2_new / second_fix) + 1e-08)
    master_new = master - 0.01 * (update + 0.1 * master)
    return (master_new, moment1_new, moment2_new)


def rotation(positions):
    half = HEAD // 2
    freqs = jnp.exp(jnp.arange(half, dtype=jnp.float32) * (-math.log(1000000.0) / half))
    angles = positions[:, :, None].astype(jnp.float32) * freqs
    cosine, sine = jnp.cos(angles), jnp.sin(angles)
    return jnp.concatenate([cosine, cosine], axis=-1), jnp.concatenate([-sine, sine], axis=-1)


def pack_kernel(query_ref, key_ref, value_ref, first_ref, second_ref):
    for member in range(8):
        start = member * 1024
        own = slice(member * 128, member * 128 + 128)
        first_ref[member, :, 0:PART] = query_ref[:, start : start + PART]
        first_ref[member, :, PART : PART + 128] = key_ref[:, own]
        first_ref[member, :, PART + 128 : FIRST] = value_ref[:, own]
        second_ref[member] = query_ref[:, start + PART : start + 1024]


def pack_columns(q_weight, keys, values):
    rows = q_weight.shape[0]
    whole = pl.BlockSpec(memory_space=pltpu.VMEM)
    return pl.pallas_call(
        pack_kernel,
        in_specs=[whole] * 3,
        out_specs=[whole] * 2,
        out_shape=[
            jax.ShapeDtypeStruct((8, rows, FIRST), jnp.bfloat16),
            jax.ShapeDtypeStruct((8, rows, PART), jnp.bfloat16),
        ],
        compiler_params=pltpu.CompilerParams(vmem_limit_bytes=16 << 20),
        cost_estimate=pl.CostEstimate(flops=0, bytes_accessed=3 << 20, transcendentals=0),
    )(q_weight, keys, values)


def project_kernel(place_ref, *refs):
    blocks, w_ref, mine_ref, other_ref, tokens_ref, held, total, sems = refs[:10], *refs[10:17]
    half = TOKENS // 2
    width = w_ref.shape[1]
    columns = mine_ref.shape[1] - 128
    keep = pltpu.make_async_copy(held, tokens_ref, sems.at[10])
    step = pl.program_id(0)

    @pl.when(step == 0)
    def _():
        copies = []
        for index in range(10):
            member = index if index < 6 else 6 + (index - 6) // 2
            features = pl.ds(pl.multiple_of(place_ref[member] * HALF, HALF), HALF)
            if index < 6:
                target = held.at[:, features]
            else:
                target = held.at[pl.ds((index - 6) % 2 * half, half), features]
            copies.append(pltpu.make_async_copy(blocks[index], target, sems.at[index]))
        for copy in copies:
            copy.start()
        for copy in copies:
            copy.wait()
        keep.start()

    xh = place_ref[8]
    own = pl.ds(pl.multiple_of(xh * half, half), half)
    partner = pl.ds(pl.multiple_of((1 - xh) * half, half), half)
    tile = pl.ds(pl.multiple_of(step * width, width), width)
    total[...] = jnp.dot(held[...], w_ref[...], preferred_element_type=jnp.float32)
    other_ref[:, tile] = total[partner, :].astype(jnp.bfloat16)
    mine_ref[:, tile] = total[own, :]

    @pl.when(step == 0)
    def _():
        def sums(rows):
            parts = jnp.zeros((half, 128), jnp.float32)
            for start in range(0, 8 * HALF, 128):
                part = held[rows, start : start + 128].astype(jnp.float32)
                parts += part * part
            return jnp.sum(parts, axis=1, keepdims=True)

        mine_ref[:, columns:] = jnp.broadcast_to(sums(own), (half, 128))
        partner_sums = sums(partner)
        high = partner_sums.astype(jnp.bfloat16).astype(jnp.float32)
        lanes = lax.broadcasted_iota(jnp.int32, (half, 128), 1)
        other_ref[:, columns:] = jnp.where(lanes < 64, high, partner_sums - high).astype(
            jnp.bfloat16
        )

    @pl.when(step == pl.num_programs(0) - 1)
    def _():
        keep.wait()


def project(place, blocks, weights):
    half = TOKENS // 2
    columns = weights.shape[1]
    width = columns + 128
    anywhere = pl.BlockSpec(memory_space=pltpu.HBM)
    return pl.pallas_call(
        project_kernel,
        grid_spec=pltpu.PrefetchScalarGridSpec(
            num_scalar_prefetch=1,
            grid=(columns // 256,),
            in_specs=[anywhere] * 10 + [pl.BlockSpec((8 * HALF, 256), lambda n, place: (0, n))],
            out_specs=[
                pl.BlockSpec((half, width), lambda n, place: (0, 0)),
                pl.BlockSpec((half, width), lambda n, place: (0, 0)),
                anywhere,
            ],
            scratch_shapes=[
                pltpu.VMEM((TOKENS, 8 * HALF), jnp.bfloat16),
                pltpu.VMEM((TOKENS, 256), jnp.float32),
                pltpu.SemaphoreType.DMA((11,)),
            ],
        ),
        out_shape=[
            jax.ShapeDtypeStruct((half, width), jnp.float32),
            jax.ShapeDtypeStruct((half, width), jnp.bfloat16),
            jax.ShapeDtypeStruct((TOKENS, 8 * HALF), jnp.bfloat16),
        ],
        compiler_params=pltpu.CompilerParams(vmem_limit_bytes=60 << 20),
        cost_estimate=pl.CostEstimate(
            flops=2 * TOKENS * 4096 * columns, bytes_accessed=12 << 20, transcendentals=0
        ),
    )(place, *blocks, weights)


def hold_kernel(keys, values, keys_out, values_out, sems):
    copies = []
    for index in range(5):
        rows = pl.ds(index * 32, 32)
        copies.append(pltpu.make_async_copy(keys.at[rows], keys_out.at[rows], sems.at[index]))
        copies.append(
            pltpu.make_async_copy(values.at[rows], values_out.at[rows], sems.at[5 + index])
        )
    for copy in copies:
        copy.start()
    for copy in copies:
        copy.wait()


def hold(k_cache, v_cache):
    far = pl.BlockSpec(memory_space=pltpu.HBM)
    near = pl.BlockSpec(memory_space=pltpu.VMEM)
    return pl.pallas_call(
        hold_kernel,
        in_specs=[far, far],
        out_specs=[near, near],
        out_shape=[jax.ShapeDtypeStruct(k_cache.shape, k_cache.dtype)] * 2,
        scratch_shapes=[pltpu.SemaphoreType.DMA((10,))],
        compiler_params=pltpu.CompilerParams(vmem_limit_bytes=12 << 20),
        cost_estimate=pl.CostEstimate(flops=0, bytes_accessed=20 << 20, transcendentals=0),
    )(k_cache, v_cache)


BLOCK = 80


def spread(scratch, array):
    for index in range(8):
        scratch[pl.ds(index, BLOCK, stride=8), :] = array
    return scratch[...].reshape(BLOCK, 8, HEAD)


def attend_kernel(first, *refs):
    if first:
        mine, came, bias, cosine, sine, mask, k_ref, v_ref = refs[:8]
        out, keys_out, values_out, scale_out = refs[8:12]
        work = refs[12]
        spare = refs[13:]
    else:
        mine, came, bias, cosine, sine, mask, k_ref, v_ref = refs[:8]
        keys_in, values_in, scale_in = refs[8:11]
        out = refs[12]
        work = refs[13]
        spare = refs[14:]

    def rotated(field, step):
        return field * cosine[step] + pltpu.roll(field, HEAD // 2, 1) * sine[step]

    def raw(step, start, scale):
        features = slice(start, start + HEAD)
        total = mine[step, :, features] + came[step, :, features].astype(jnp.float32)
        return total * scale + bias[:, features]

    new_keys, new_values = [], []
    for step in range(2):
        if first:
            part = came[step, :, FIRST : FIRST + 128].astype(jnp.float32)
            sums = mine[step, :, FIRST : FIRST + 128] + part + pltpu.roll(part, 64, 1)
            scale = lax.rsqrt(sums / D + 1e-06) / math.sqrt(D)
            scale_out[step] = scale
            key = rotated(raw(step, PART, scale), step).astype(jnp.bfloat16)
            value = raw(step, PART + HEAD, scale).astype(jnp.bfloat16)
            keys_out[step] = key
            values_out[step] = value
        else:
            scale = scale_in[step]
            key, value = keys_in[step], values_in[step]
        new_keys.append(key.astype(jnp.float32))
        new_values.append(value.astype(jnp.float32))
        for head in range(4):
            query = rotated(raw(step, head * HEAD, scale), step)
            work[pl.ds(step * 4 + head, BLOCK, stride=8), :] = query
    queries = work[...].reshape(BLOCK, 8, HEAD).astype(jnp.bfloat16)
    wide = queries.astype(jnp.float32)
    root = 1.0 / math.sqrt(HEAD)
    near = pl.ds(pl.multiple_of(pl.program_id(0) * BLOCK, BLOCK), BLOCK)
    scores = (
        lax.dot_general(
            queries, k_ref[near], (((2,), (2,)), ((0,), (0,))), preferred_element_type=jnp.float32
        )
        * root
        + mask[...]
    )
    second = lax.broadcasted_iota(jnp.int32, (BLOCK, 8, 1), 1) >= 4
    own = [
        jnp.sum(wide * spread(spare[u], new_keys[u]), axis=2, keepdims=True) * root
        for u in range(2)
    ]
    own[1] = jnp.where(second, own[1], -1e30)
    peak = jnp.maximum(
        jnp.max(scores, axis=2, keepdims=True), jnp.maximum(own[0], own[1])
    )
    shares = jnp.exp(scores - peak)
    own = [jnp.exp(score - peak) for score in own]
    total = jnp.sum(shares, axis=2, keepdims=True) + own[0] + own[1]
    inverse = 1.0 / total
    weights = (shares * inverse).astype(jnp.bfloat16)
    context = lax.dot_general(
        weights, v_ref[near], (((2,), (1,)), ((0,), (0,))), preferred_element_type=jnp.float32
    )
    for u in range(2):
        weight = (own[u] * inverse).astype(jnp.bfloat16).astype(jnp.float32)
        context += weight * spread(spare[2 + u], new_values[u])
    work[...] = context.reshape(BLOCK * 8, HEAD)
    for step in range(2):
        for head in range(4):
            result = work[pl.ds(step * 4 + head, BLOCK, stride=8), :]
            out[step, :, head * HEAD : (head + 1) * HEAD] = result.astype(jnp.bfloat16)


def attend(first, mine, came, bias, cosine, sine, mask, k_cache, v_cache, *more):
    width = mine.shape[-1]

    def steps(columns):
        return pl.BlockSpec((2, BLOCK, columns), lambda i: (0, i, 0))

    def rows(a, b):
        return pl.BlockSpec((BLOCK, a, b), lambda i: (i, 0, 0))

    in_specs = [
        steps(width),
        steps(width),
        pl.BlockSpec((1, bias.shape[-1]), lambda i: (0, 0)),
        steps(HEAD),
        steps(HEAD),
        rows(8, HEAD),
        pl.BlockSpec(memory_space=pltpu.VMEM),
        pl.BlockSpec(memory_space=pltpu.VMEM),
    ]
    context = jax.ShapeDtypeStruct((2, ROWS, 2 * PART), jnp.bfloat16)
    if first:
        out_specs = [steps(PART), steps(HEAD), steps(HEAD), steps(HEAD)]
        out_shape = [
            context,
            jax.ShapeDtypeStruct((2, ROWS, HEAD), jnp.bfloat16),
            jax.ShapeDtypeStruct((2, ROWS, HEAD), jnp.bfloat16),
            jax.ShapeDtypeStruct((2, ROWS, HEAD), jnp.float32),
        ]
        aliases = {}
    else:
        in_specs += [steps(HEAD), steps(HEAD), steps(HEAD), pl.BlockSpec(memory_space=pl.ANY)]
        out_specs = pl.BlockSpec((2, BLOCK, PART), lambda i: (0, i, 1))
        out_shape = context
        aliases = {11: 0}
    return pl.pallas_call(
        functools.partial(attend_kernel, first),
        grid=(ROWS // BLOCK,),
        in_specs=in_specs,
        out_specs=out_specs,
        out_shape=out_shape,
        scratch_shapes=[pltpu.VMEM((BLOCK * 8, HEAD), jnp.float32)] * 5,
        input_output_aliases=aliases,
        compiler_params=pltpu.CompilerParams(vmem_limit_bytes=24 << 20),
        cost_estimate=pl.CostEstimate(
            flops=4 * ROWS * 8 * 128 * 128, bytes_accessed=12 << 20, transcendentals=ROWS * 1024
        ),
    )(mine, came, bias, cosine, sine, mask, k_cache, v_cache, *more)


def per_device(
    token_ids,
    embedding,
    cache_lengths,
    q_weight,
    q_bias,
    kv_bias,
    kv_master,
    kv_moment1,
    kv_moment2,
    kv_grad,
    k_cache,
    v_cache,
):
    xh, z, c = (lax.axis_index(name) for name in FSDP)
    y, xl = (lax.axis_index(name) for name in TP)
    fsdp_index = (xh * 4 + z) * 2 + c
    pair = z * 2 + c
    vocab_rows = embedding.shape[0]

    queries = send(q_weight, swap_xh_core)
    master_new, moment1_new, moment2_new = adamw_update(kv_master, kv_moment1, kv_moment2, kv_grad)
    rollout = master_new.astype(jnp.bfloat16)
    rollout = jnp.concatenate([rollout[:, 0, :], rollout[:, 1, :]], axis=1)
    rollout = send(rollout, swap_xh_core)

    paired = token_ids.reshape(2, 2, PAIRS, ROWS).transpose(2, 1, 0, 3).reshape(PAIRS, TOKENS)
    owners = paired // vocab_rows
    order = jnp.arange(TOKENS, dtype=jnp.int32)
    earlier = order[:, None] < order[None, :]
    same_id = paired[:, :, None] == paired[:, None, :]
    first = ~jnp.any(same_id & earlier[None], axis=1)
    counts = jnp.sum(
        (first[:, None, :] & (owners[:, None, :] == jnp.arange(OWNERS)[None, :, None])).astype(
            jnp.int32
        ),
        axis=2,
    )
    rounds = (jnp.max(counts) + SLOTS - 1) // SLOTS

    def ranks_in(chosen):
        return jnp.dot(
            chosen.astype(jnp.bfloat16),
            earlier.astype(jnp.bfloat16),
            preferred_element_type=jnp.float32,
        ).astype(jnp.int32)

    local = paired - fsdp_index * vocab_rows
    sent = first & (owners == fsdp_index)
    sent_rank = jnp.where(sent, ranks_in(sent), -1)
    own_ids = lax.dynamic_index_in_dim(paired, pair, 0, keepdims=False)
    own_first = lax.dynamic_index_in_dim(first, pair, 0, keepdims=False)
    own_owners = lax.dynamic_index_in_dim(owners, pair, 0, keepdims=False)
    by_owner = own_first[None, :] & (own_owners[None, :] == jnp.arange(OWNERS)[:, None])
    own_ranks = jnp.sum(jnp.where(by_owner, ranks_in(by_owner), 0), axis=0)
    got_rank = jnp.sum(
        jnp.where(
            (own_ids[:, None] == own_ids[None, :]) & own_first[:, None], own_ranks[:, None], 0
        ),
        axis=0,
    )

    def wanted_rows(turn):
        slots = turn * SLOTS + jnp.arange(SLOTS, dtype=jnp.int32)
        wanted = jnp.sum(
            jnp.where(sent_rank[:, :, None] == slots[None, None, :], local[:, :, None], 0), axis=1
        )
        wanted = lax.optimization_barrier(wanted)
        rows = embedding.at[wanted.reshape(-1)].get(mode="promise_in_bounds")
        rows = rows.reshape(PAIRS, SLOTS, 2, HALF).transpose(2, 0, 1, 3)
        return rows.reshape(OWNERS, SLOTS, HALF)

    def exchanged(rows):
        return lax.all_to_all(rows, FSDP, split_axis=0, concat_axis=0)

    def placed_rows(turn, rows):
        slot = got_rank - turn * SLOTS
        inside = (slot >= 0) & (slot < SLOTS)
        spot = jnp.where(inside, own_owners * SLOTS + slot, -1)
        pick = spot[:, None] == jnp.arange(OWNERS * SLOTS, dtype=jnp.int32)[None, :]
        return jnp.dot(
            pick.astype(jnp.bfloat16),
            rows.reshape(OWNERS * SLOTS, HALF),
            preferred_element_type=jnp.float32,
        ).astype(jnp.bfloat16)

    rows = exchanged(wanted_rows(0))
    queries, rollout, rows = lax.optimization_barrier((queries, rollout, rows))
    first_part, second_part = pack_columns(queries, rollout[:, :1024], rollout[:, 1024:])

    def gathered(part):
        part = lax.all_to_all(part, TP, split_axis=0, concat_axis=0)
        part = lax.all_gather(part.reshape(HALF, part.shape[-1]), ("z", "c"))
        return part.reshape(8 * HALF, part.shape[-1])

    weights = [gathered(first_part), gathered(second_part)]
    own = placed_rows(0, rows)
    _, own = lax.while_loop(
        lambda state: state[0] < rounds,
        lambda state: (state[0] + 1, state[1] + placed_rows(state[0], exchanged(wanted_rows(state[0])))),
        (jnp.int32(1), own),
    )

    half = TOKENS // 2
    across = send(own, other_xl)
    below = send(own, along_y(1))
    above = send(own, along_y(-1))
    far_low = send(below[:half], along_y(1))
    far_high = send(above[half:], along_y(-1))
    below_across = send(across, along_y(1))
    above_across = send(across, along_y(-1))
    far_low_across = send(far_low, other_xl)
    far_high_across = send(far_high, other_xl)
    members = [
        y * 2 + xl,
        y * 2 + 1 - xl,
        (y + 3) % 4 * 2 + xl,
        (y + 1) % 4 * 2 + xl,
        (y + 3) % 4 * 2 + 1 - xl,
        (y + 1) % 4 * 2 + 1 - xl,
        (y + 2) % 4 * 2 + xl,
        (y + 2) % 4 * 2 + 1 - xl,
    ]
    place = jnp.stack([member % 4 * 2 + member // 4 for member in members] + [xh]).astype(jnp.int32)
    blocks = (
        own,
        across,
        below,
        above,
        below_across,
        above_across,
        far_low,
        far_high,
        far_low_across,
        far_high_across,
    )
    mine_first, other_first, tokens = project(place, blocks, weights[0])
    came_first = send(other_first, other_xh)
    k_cache, v_cache, _ = lax.optimization_barrier((k_cache, v_cache, other_first))
    k_cache, v_cache = hold(k_cache, v_cache)
    total_second = jnp.dot(tokens, weights[1], preferred_element_type=jnp.float32)
    mine_second = lax.dynamic_slice_in_dim(total_second, xh * half, half, 0)
    other_second = lax.dynamic_slice_in_dim(total_second, (1 - xh) * half, half, 0)
    came_second = send(other_second.astype(jnp.bfloat16), other_xh)

    cosine, sine = rotation(cache_lengths[None, :] + jnp.arange(2, dtype=jnp.int32)[:, None])
    inside = jnp.arange(HEAD, dtype=jnp.int32)[None, :] < cache_lengths[:, None]
    mask = jnp.where(inside, 0.0, -1e30).astype(jnp.float32)
    mask = jnp.broadcast_to(mask[:, None, :], (ROWS, 8, HEAD))
    wide = q_bias.astype(jnp.float32)
    bias_first = jnp.concatenate([wide[:PART], kv_bias.reshape(256).astype(jnp.float32)])

    def stepwise(array):
        return array.reshape(2, ROWS, array.shape[-1])

    context, keys, values, scale = attend(
        True,
        stepwise(mine_first),
        stepwise(came_first),
        bias_first[None],
        cosine,
        sine,
        mask,
        k_cache,
        v_cache,
    )
    context = attend(
        False,
        stepwise(mine_second),
        stepwise(came_second),
        wide[None, PART:],
        cosine,
        sine,
        mask,
        k_cache,
        v_cache,
        keys,
        values,
        scale,
        context,
    )
    return (context, master_new, moment1_new, moment2_new)


def solution(mesh):
    parts = Mesh(mesh.devices.reshape(SIZES), NAMES)
    placed = (
        P(),
        P(FSDP, TP),
        P(FSDP),
        P(NAMES, None),
        P(TP),
        P(None, TP),
        P(NAMES, None, None),
        P(NAMES, None, None),
        P(NAMES, None, None),
        P(NAMES, None, None),
        P(FSDP, None, TP),
        P(FSDP, None, TP),
    )
    return jax.shard_map(
        per_device,
        mesh=parts,
        in_specs=placed,
        out_specs=(
            P(None, FSDP, TP),
            P(NAMES, None, None),
            P(NAMES, None, None),
            P(NAMES, None, None),
        ),
        check_vma=False,
    )
```

```python
import functools
import functools
import math

import jax
import jax.numpy as jnp
from jax import lax
from jax.experimental import pallas as pl
from jax.experimental.pallas import tpu as pltpu
from jax.sharding import Mesh
from jax.sharding import PartitionSpec as P

D = 8192
HEAD = 128
ADAM_STEP = 10

NAMES = ("xh", "z", "c", "y", "xl")
SIZES = (2, 4, 2, 4, 2)
FSDP = ("xh", "z", "c")
TP = ("y", "xl")
OWNERS = 16
PAIRS = 8
ROWS = 160
TOKENS = 4 * ROWS
HALF = 512
SLOTS = 56
PART = 512
FIRST = 768


def pairs_of(move):
    found = []
    total = math.prod(SIZES)
    for index in range(total):
        rest, coords = index, []
        for size in reversed(SIZES):
            coords.append(rest % size)
            rest //= size
        target = 0
        for value, size in zip(move(*reversed(coords)), SIZES):
            target = target * size + value
        found.append((index, target))
    return found


def send(array, move):
    return lax.ppermute(array, NAMES, pairs_of(move))


def along_y(step):
    return lambda xh, z, c, y, xl: (xh, z, c, (y + step) % 4, xl)


def other_xl(xh, z, c, y, xl):
    return (xh, z, c, y, 1 - xl)


def other_xh(xh, z, c, y, xl):
    return (1 - xh, z, c, y, xl)


def swap_xh_core(xh, z, c, y, xl):
    return (c, z, xh, y, xl)


def adamw_update(master, moment1, moment2, gradient):
    gradient = gradient.astype(jnp.float32)
    moment1_new = 0.9 * moment1 + 0.1 * gradient
    moment2_new = 0.95 * moment2 + 0.05 * gradient * gradient
    first_fix = 1.0 - 0.9**ADAM_STEP
    second_fix = 1.0 - 0.95**ADAM_STEP
    update = moment1_new / first_fix / (jnp.sqrt(moment2_new / second_fix) + 1e-08)
    master_new = master - 0.01 * (update + 0.1 * master)
    return (master_new, moment1_new, moment2_new)


def rotation(positions):
    half = HEAD // 2
    freqs = jnp.exp(jnp.arange(half, dtype=jnp.float32) * (-math.log(1000000.0) / half))
    angles = positions[:, :, None].astype(jnp.float32) * freqs
    cosine, sine = jnp.cos(angles), jnp.sin(angles)
    return jnp.concatenate([cosine, cosine], axis=-1), jnp.concatenate([-sine, sine], axis=-1)


def pack_kernel(query_ref, key_ref, value_ref, first_ref, second_ref):
    for member in range(8):
        start = member * 1024
        own = slice(member * 128, member * 128 + 128)
        first_ref[member, :, 0:PART] = query_ref[:, start : start + PART]
        first_ref[member, :, PART : PART + 128] = key_ref[:, own]
        first_ref[member, :, PART + 128 : FIRST] = value_ref[:, own]
        second_ref[member] = query_ref[:, start + PART : start + 1024]


def pack_columns(q_weight, keys, values):
    rows = q_weight.shape[0]
    whole = pl.BlockSpec(memory_space=pltpu.VMEM)
    return pl.pallas_call(
        pack_kernel,
        in_specs=[whole] * 3,
        out_specs=[whole] * 2,
        out_shape=[
            jax.ShapeDtypeStruct((8, rows, FIRST), jnp.bfloat16),
            jax.ShapeDtypeStruct((8, rows, PART), jnp.bfloat16),
        ],
        compiler_params=pltpu.CompilerParams(vmem_limit_bytes=16 << 20),
        cost_estimate=pl.CostEstimate(flops=0, bytes_accessed=3 << 20, transcendentals=0),
    )(q_weight, keys, values)


def project_kernel(place_ref, *refs):
    blocks, w_ref, mine_ref, other_ref, tokens_ref, held, total, sems = refs[:10], *refs[10:17]
    half = TOKENS // 2
    width = w_ref.shape[1]
    columns = mine_ref.shape[1] - 128
    keep = pltpu.make_async_copy(held, tokens_ref, sems.at[10])
    step = pl.program_id(0)

    @pl.when(step == 0)
    def _():
        copies = []
        for index in range(10):
            member = index if index < 6 else 6 + (index - 6) // 2
            features = pl.ds(pl.multiple_of(place_ref[member] * HALF, HALF), HALF)
            if index < 6:
                target = held.at[:, features]
            else:
                target = held.at[pl.ds((index - 6) % 2 * half, half), features]
            copies.append(pltpu.make_async_copy(blocks[index], target, sems.at[index]))
        for copy in copies:
            copy.start()
        for copy in copies:
            copy.wait()
        keep.start()

    xh = place_ref[8]
    own = pl.ds(pl.multiple_of(xh * half, half), half)
    partner = pl.ds(pl.multiple_of((1 - xh) * half, half), half)
    tile = pl.ds(pl.multiple_of(step * width, width), width)
    total[...] = jnp.dot(held[...], w_ref[...], preferred_element_type=jnp.float32)
    other_ref[:, tile] = total[partner, :].astype(jnp.bfloat16)
    mine_ref[:, tile] = total[own, :]

    @pl.when(step == 0)
    def _():
        def sums(rows):
            parts = jnp.zeros((half, 128), jnp.float32)
            for start in range(0, 8 * HALF, 128):
                part = held[rows, start : start + 128].astype(jnp.float32)
                parts += part * part
            return jnp.sum(parts, axis=1, keepdims=True)

        mine_ref[:, columns:] = jnp.broadcast_to(sums(own), (half, 128))
        partner_sums = sums(partner)
        high = partner_sums.astype(jnp.bfloat16).astype(jnp.float32)
        lanes = lax.broadcasted_iota(jnp.int32, (half, 128), 1)
        other_ref[:, columns:] = jnp.where(lanes < 64, high, partner_sums - high).astype(
            jnp.bfloat16
        )

    @pl.when(step == pl.num_programs(0) - 1)
    def _():
        keep.wait()


def project(place, blocks, weights):
    half = TOKENS // 2
    columns = weights.shape[1]
    width = columns + 128
    anywhere = pl.BlockSpec(memory_space=pltpu.HBM)
    return pl.pallas_call(
        project_kernel,
        grid_spec=pltpu.PrefetchScalarGridSpec(
            num_scalar_prefetch=1,
            grid=(columns // 256,),
            in_specs=[anywhere] * 10 + [pl.BlockSpec((8 * HALF, 256), lambda n, place: (0, n))],
            out_specs=[
                pl.BlockSpec((half, width), lambda n, place: (0, 0)),
                pl.BlockSpec((half, width), lambda n, place: (0, 0)),
                anywhere,
            ],
            scratch_shapes=[
                pltpu.VMEM((TOKENS, 8 * HALF), jnp.bfloat16),
                pltpu.VMEM((TOKENS, 256), jnp.float32),
                pltpu.SemaphoreType.DMA((11,)),
            ],
        ),
        out_shape=[
            jax.ShapeDtypeStruct((half, width), jnp.float32),
            jax.ShapeDtypeStruct((half, width), jnp.bfloat16),
            jax.ShapeDtypeStruct((TOKENS, 8 * HALF), jnp.bfloat16),
        ],
        compiler_params=pltpu.CompilerParams(vmem_limit_bytes=60 << 20),
        cost_estimate=pl.CostEstimate(
            flops=2 * TOKENS * 4096 * columns, bytes_accessed=12 << 20, transcendentals=0
        ),
    )(place, *blocks, weights)


def hold_kernel(keys, values, keys_out, values_out, sems):
    copies = []
    for index in range(5):
        rows = pl.ds(index * 32, 32)
        copies.append(pltpu.make_async_copy(keys.at[rows], keys_out.at[rows], sems.at[index]))
        copies.append(
            pltpu.make_async_copy(values.at[rows], values_out.at[rows], sems.at[5 + index])
        )
    for copy in copies:
        copy.start()
    for copy in copies:
        copy.wait()


def hold(k_cache, v_cache):
    far = pl.BlockSpec(memory_space=pltpu.HBM)
    near = pl.BlockSpec(memory_space=pltpu.VMEM)
    return pl.pallas_call(
        hold_kernel,
        in_specs=[far, far],
        out_specs=[near, near],
        out_shape=[jax.ShapeDtypeStruct(k_cache.shape, k_cache.dtype)] * 2,
        scratch_shapes=[pltpu.SemaphoreType.DMA((10,))],
        compiler_params=pltpu.CompilerParams(vmem_limit_bytes=12 << 20),
        cost_estimate=pl.CostEstimate(flops=0, bytes_accessed=20 << 20, transcendentals=0),
    )(k_cache, v_cache)


BLOCK = 160


def spread(scratch, array):
    for index in range(8):
        scratch[pl.ds(index, BLOCK, stride=8), :] = array
    return scratch[...].reshape(BLOCK, 8, HEAD)


def attend_kernel(first, *refs):
    if first:
        mine, came, bias, cosine, sine, mask, k_ref, v_ref = refs[:8]
        out, keys_out, values_out, scale_out = refs[8:12]
        work = refs[12]
        spare = refs[13:]
    else:
        mine, came, bias, cosine, sine, mask, k_ref, v_ref = refs[:8]
        keys_in, values_in, scale_in = refs[8:11]
        out = refs[12]
        work = refs[13]
        spare = refs[14:]

    def rotated(field, step):
        return field * cosine[step] + pltpu.roll(field, HEAD // 2, 1) * sine[step]

    def raw(step, start, scale):
        features = slice(start, start + HEAD)
        total = mine[step, :, features] + came[step, :, features].astype(jnp.float32)
        return total * scale + bias[:, features]

    new_keys, new_values = [], []
    for step in range(2):
        if first:
            part = came[step, :, FIRST : FIRST + 128].astype(jnp.float32)
            sums = mine[step, :, FIRST : FIRST + 128] + part + pltpu.roll(part, 64, 1)
            scale = lax.rsqrt(sums / D + 1e-06) / math.sqrt(D)
            scale_out[step] = scale
            key = rotated(raw(step, PART, scale), step).astype(jnp.bfloat16)
            value = raw(step, PART + HEAD, scale).astype(jnp.bfloat16)
            keys_out[step] = key
            values_out[step] = value
        else:
            scale = scale_in[step]
            key, value = keys_in[step], values_in[step]
        new_keys.append(key.astype(jnp.float32))
        new_values.append(value.astype(jnp.float32))
        for head in range(4):
            query = rotated(raw(step, head * HEAD, scale), step)
            work[pl.ds(step * 4 + head, BLOCK, stride=8), :] = query
    queries = work[...].reshape(BLOCK, 8, HEAD).astype(jnp.bfloat16)
    wide = queries.astype(jnp.float32)
    root = 1.0 / math.sqrt(HEAD)
    near = pl.ds(pl.multiple_of(pl.program_id(0) * BLOCK, BLOCK), BLOCK)
    scores = (
        lax.dot_general(
            queries, k_ref[near], (((2,), (2,)), ((0,), (0,))), preferred_element_type=jnp.float32
        )
        * root
        + mask[...]
    )
    second = lax.broadcasted_iota(jnp.int32, (BLOCK, 8, 1), 1) >= 4
    own = [
        jnp.sum(wide * spread(spare[u], new_keys[u]), axis=2, keepdims=True) * root
        for u in range(2)
    ]
    own[1] = jnp.where(second, own[1], -1e30)
    peak = jnp.maximum(
        jnp.max(scores, axis=2, keepdims=True), jnp.maximum(own[0], own[1])
    )
    shares = jnp.exp(scores - peak)
    own = [jnp.exp(score - peak) for score in own]
    total = jnp.sum(shares, axis=2, keepdims=True) + own[0] + own[1]
    inverse = 1.0 / total
    weights = (shares * inverse).astype(jnp.bfloat16)
    context = lax.dot_general(
        weights, v_ref[near], (((2,), (1,)), ((0,), (0,))), preferred_element_type=jnp.float32
    )
    for u in range(2):
        weight = (own[u] * inverse).astype(jnp.bfloat16).astype(jnp.float32)
        context += weight * spread(spare[2 + u], new_values[u])
    work[...] = context.reshape(BLOCK * 8, HEAD)
    for step in range(2):
        for head in range(4):
            result = work[pl.ds(step * 4 + head, BLOCK, stride=8), :]
            out[step, :, head * HEAD : (head + 1) * HEAD] = result.astype(jnp.bfloat16)


def attend(first, mine, came, bias, cosine, sine, mask, k_cache, v_cache, *more):
    width = mine.shape[-1]

    def steps(columns):
        return pl.BlockSpec((2, BLOCK, columns), lambda i: (0, i, 0))

    def rows(a, b):
        return pl.BlockSpec((BLOCK, a, b), lambda i: (i, 0, 0))

    in_specs = [
        steps(width),
        steps(width),
        pl.BlockSpec((1, bias.shape[-1]), lambda i: (0, 0)),
        steps(HEAD),
        steps(HEAD),
        rows(8, HEAD),
        pl.BlockSpec(memory_space=pltpu.VMEM),
        pl.BlockSpec(memory_space=pltpu.VMEM),
    ]
    context = jax.ShapeDtypeStruct((2, ROWS, 2 * PART), jnp.bfloat16)
    if first:
        out_specs = [steps(PART), steps(HEAD), steps(HEAD), steps(HEAD)]
        out_shape = [
            context,
            jax.ShapeDtypeStruct((2, ROWS, HEAD), jnp.bfloat16),
            jax.ShapeDtypeStruct((2, ROWS, HEAD), jnp.bfloat16),
            jax.ShapeDtypeStruct((2, ROWS, HEAD), jnp.float32),
        ]
        aliases = {}
    else:
        in_specs += [steps(HEAD), steps(HEAD), steps(HEAD), pl.BlockSpec(memory_space=pl.ANY)]
        out_specs = pl.BlockSpec((2, BLOCK, PART), lambda i: (0, i, 1))
        out_shape = context
        aliases = {11: 0}
    return pl.pallas_call(
        functools.partial(attend_kernel, first),
        grid=(ROWS // BLOCK,),
        in_specs=in_specs,
        out_specs=out_specs,
        out_shape=out_shape,
        scratch_shapes=[pltpu.VMEM((BLOCK * 8, HEAD), jnp.float32)] * 5,
        input_output_aliases=aliases,
        compiler_params=pltpu.CompilerParams(vmem_limit_bytes=24 << 20),
        cost_estimate=pl.CostEstimate(
            flops=4 * ROWS * 8 * 128 * 128, bytes_accessed=12 << 20, transcendentals=ROWS * 1024
        ),
    )(mine, came, bias, cosine, sine, mask, k_cache, v_cache, *more)


def per_device(
    token_ids,
    embedding,
    cache_lengths,
    q_weight,
    q_bias,
    kv_bias,
    kv_master,
    kv_moment1,
    kv_moment2,
    kv_grad,
    k_cache,
    v_cache,
):
    xh, z, c = (lax.axis_index(name) for name in FSDP)
    y, xl = (lax.axis_index(name) for name in TP)
    fsdp_index = (xh * 4 + z) * 2 + c
    pair = z * 2 + c
    vocab_rows = embedding.shape[0]

    queries = send(q_weight, swap_xh_core)
    master_new, moment1_new, moment2_new = adamw_update(kv_master, kv_moment1, kv_moment2, kv_grad)
    rollout = master_new.astype(jnp.bfloat16)
    rollout = jnp.concatenate([rollout[:, 0, :], rollout[:, 1, :]], axis=1)
    rollout = send(rollout, swap_xh_core)

    paired = token_ids.reshape(2, 2, PAIRS, ROWS).transpose(2, 1, 0, 3).reshape(PAIRS, TOKENS)
    owners = paired // vocab_rows
    order = jnp.arange(TOKENS, dtype=jnp.int32)
    earlier = order[:, None] < order[None, :]
    same_id = paired[:, :, None] == paired[:, None, :]
    first = ~jnp.any(same_id & earlier[None], axis=1)
    counts = jnp.sum(
        (first[:, None, :] & (owners[:, None, :] == jnp.arange(OWNERS)[None, :, None])).astype(
            jnp.int32
        ),
        axis=2,
    )
    rounds = (jnp.max(counts) + SLOTS - 1) // SLOTS

    def ranks_in(chosen):
        return jnp.dot(
            chosen.astype(jnp.bfloat16),
            earlier.astype(jnp.bfloat16),
            preferred_element_type=jnp.float32,
        ).astype(jnp.int32)

    local = paired - fsdp_index * vocab_rows
    sent = first & (owners == fsdp_index)
    sent_rank = jnp.where(sent, ranks_in(sent), -1)
    own_ids = lax.dynamic_index_in_dim(paired, pair, 0, keepdims=False)
    own_first = lax.dynamic_index_in_dim(first, pair, 0, keepdims=False)
    own_owners = lax.dynamic_index_in_dim(owners, pair, 0, keepdims=False)
    by_owner = own_first[None, :] & (own_owners[None, :] == jnp.arange(OWNERS)[:, None])
    own_ranks = jnp.sum(jnp.where(by_owner, ranks_in(by_owner), 0), axis=0)
    got_rank = jnp.sum(
        jnp.where(
            (own_ids[:, None] == own_ids[None, :]) & own_first[:, None], own_ranks[:, None], 0
        ),
        axis=0,
    )

    def wanted_rows(turn):
        slots = turn * SLOTS + jnp.arange(SLOTS, dtype=jnp.int32)
        wanted = jnp.sum(
            jnp.where(sent_rank[:, :, None] == slots[None, None, :], local[:, :, None], 0), axis=1
        )
        wanted = lax.optimization_barrier(wanted)
        rows = embedding.at[wanted.reshape(-1)].get(mode="promise_in_bounds")
        rows = rows.reshape(PAIRS, SLOTS, 2, HALF).transpose(2, 0, 1, 3)
        return rows.reshape(OWNERS, SLOTS, HALF)

    def exchanged(rows):
        return lax.all_to_all(rows, FSDP, split_axis=0, concat_axis=0)

    def placed_rows(turn, rows):
        slot = got_rank - turn * SLOTS
        inside = (slot >= 0) & (slot < SLOTS)
        spot = jnp.where(inside, own_owners * SLOTS + slot, -1)
        pick = spot[:, None] == jnp.arange(OWNERS * SLOTS, dtype=jnp.int32)[None, :]
        return jnp.dot(
            pick.astype(jnp.bfloat16),
            rows.reshape(OWNERS * SLOTS, HALF),
            preferred_element_type=jnp.float32,
        ).astype(jnp.bfloat16)

    rows = exchanged(wanted_rows(0))
    queries, rollout, rows = lax.optimization_barrier((queries, rollout, rows))
    first_part, second_part = pack_columns(queries, rollout[:, :1024], rollout[:, 1024:])

    def gathered(part):
        part = lax.all_to_all(part, TP, split_axis=0, concat_axis=0)
        part = lax.all_gather(part.reshape(HALF, part.shape[-1]), ("z", "c"))
        return part.reshape(8 * HALF, part.shape[-1])

    weights = [gathered(first_part), gathered(second_part)]
    own = placed_rows(0, rows)
    _, own = lax.while_loop(
        lambda state: state[0] < rounds,
        lambda state: (state[0] + 1, state[1] + placed_rows(state[0], exchanged(wanted_rows(state[0])))),
        (jnp.int32(1), own),
    )

    half = TOKENS // 2
    across = send(own, other_xl)
    below = send(own, along_y(1))
    above = send(own, along_y(-1))
    far_low = send(below[:half], along_y(1))
    far_high = send(above[half:], along_y(-1))
    below_across = send(across, along_y(1))
    above_across = send(across, along_y(-1))
    far_low_across = send(far_low, other_xl)
    far_high_across = send(far_high, other_xl)
    members = [
        y * 2 + xl,
        y * 2 + 1 - xl,
        (y + 3) % 4 * 2 + xl,
        (y + 1) % 4 * 2 + xl,
        (y + 3) % 4 * 2 + 1 - xl,
        (y + 1) % 4 * 2 + 1 - xl,
        (y + 2) % 4 * 2 + xl,
        (y + 2) % 4 * 2 + 1 - xl,
    ]
    place = jnp.stack([member % 4 * 2 + member // 4 for member in members] + [xh]).astype(jnp.int32)
    blocks = (
        own,
        across,
        below,
        above,
        below_across,
        above_across,
        far_low,
        far_high,
        far_low_across,
        far_high_across,
    )
    mine_first, other_first, tokens = project(place, blocks, weights[0])
    came_first = send(other_first, other_xh)
    k_cache, v_cache, _ = lax.optimization_barrier((k_cache, v_cache, other_first))
    k_cache, v_cache = hold(k_cache, v_cache)
    total_second = jnp.dot(tokens, weights[1], preferred_element_type=jnp.float32)
    mine_second = lax.dynamic_slice_in_dim(total_second, xh * half, half, 0)
    other_second = lax.dynamic_slice_in_dim(total_second, (1 - xh) * half, half, 0)
    came_second = send(other_second.astype(jnp.bfloat16), other_xh)

    cosine, sine = rotation(cache_lengths[None, :] + jnp.arange(2, dtype=jnp.int32)[:, None])
    inside = jnp.arange(HEAD, dtype=jnp.int32)[None, :] < cache_lengths[:, None]
    mask = jnp.where(inside, 0.0, -1e30).astype(jnp.float32)
    mask = jnp.broadcast_to(mask[:, None, :], (ROWS, 8, HEAD))
    wide = q_bias.astype(jnp.float32)
    bias_first = jnp.concatenate([wide[:PART], kv_bias.reshape(256).astype(jnp.float32)])

    def stepwise(array):
        return array.reshape(2, ROWS, array.shape[-1])

    context, keys, values, scale = attend(
        True,
        stepwise(mine_first),
        stepwise(came_first),
        bias_first[None],
        cosine,
        sine,
        mask,
        k_cache,
        v_cache,
    )
    context = attend(
        False,
        stepwise(mine_second),
        stepwise(came_second),
        wide[None, PART:],
        cosine,
        sine,
        mask,
        k_cache,
        v_cache,
        keys,
        values,
        scale,
        context,
    )
    return (context, master_new, moment1_new, moment2_new)


def solution(mesh):
    parts = Mesh(mesh.devices.reshape(SIZES), NAMES)
    placed = (
        P(),
        P(FSDP, TP),
        P(FSDP),
        P(NAMES, None),
        P(TP),
        P(None, TP),
        P(NAMES, None, None),
        P(NAMES, None, None),
        P(NAMES, None, None),
        P(NAMES, None, None),
        P(FSDP, None, TP),
        P(FSDP, None, TP),
    )
    return jax.shard_map(
        per_device,
        mesh=parts,
        in_specs=placed,
        out_specs=(
            P(None, FSDP, TP),
            P(NAMES, None, None),
            P(NAMES, None, None),
            P(NAMES, None, None),
        ),
        check_vma=False,
    )
```
